32 devices in a mesh: blk: 8 (over z, core), pack: 4 (over y, x).
Axes of the slice: x: 2, y: 2, z: 4, core: 2. Of those that a mesh axis runs over, the one named last changes fastest.
Arguments:
- tokens: bfloat16 [4, 2048, 1536], P('pack', 'blk'), may hold values from -6 to 6
- lengths: int32 [4, 8], P('pack'), may hold values from 1 to 1936, as said below
- out_grad: bfloat16 [4, 2048, 1536], P('pack', 'blk'), may hold values from -6 to 6
- w_qkv: float32 [1536, 2048], P(('blk', 'pack')), may hold values from -0.21875 to 0.21875
- b_qkv: float32 [2048], P(('blk', 'pack')), may hold values from -0.6 to 0.6
- w_out: float32 [1536, 1536], P(('blk', 'pack')), may hold values from -0.625 to 0.625
- gain_attn: float32 [1536], P(('blk', 'pack')), may hold values from 0.5 to 1.5
- w_gate: float32 [1536, 8960], P(('blk', 'pack')), may hold values from -0.15625 to 0.15625
- w_up: float32 [1536, 8960], P(('blk', 'pack')), may hold values from -0.15625 to 0.15625
- w_down: float32 [8960, 1536], P(('blk', 'pack')), may hold values from -0.0625 to 0.0625
- gain_mlp: float32 [1536], P(('blk', 'pack')), may hold values from 0.5 to 1.5
Outputs:
- output: bfloat16 [4, 2048, 1536], P('pack', 'blk')
- tokens_grad: bfloat16 [4, 2048, 1536], P('pack', 'blk')
- grad_w_qkv: float32 [1536, 2048], P(('blk', 'pack'))
- grad_b_qkv: float32 [2048], P(('blk', 'pack'))
- grad_w_out: float32 [1536, 1536], P(('blk', 'pack'))
- grad_gain_attn: float32 [1536], P(('blk', 'pack'))
- grad_w_gate: float32 [1536, 8960], P(('blk', 'pack'))
- grad_w_up: float32 [1536, 8960], P(('blk', 'pack'))
- grad_w_down: float32 [8960, 1536], P(('blk', 'pack'))
- grad_gain_mlp: float32 [1536], P(('blk', 'pack'))
The draws below stay inside these ranges and needn't reach their ends.
Inputs may be any that keep to these rules, and one draw needn't show every extreme that they name: In each pack the 8 lengths sum to 2048; exactly one document starts within the first 256 tokens and ends within the last 256 tokens, and the other documents together hold fewer than 256 tokens and lie within the first or the last 256 tokens.
All inputs are finite; a program needn't handle non-finite values.
Results may differ from the reference program's by a relative error of at most 0.018.
The reference program's roundings to bfloat16 on the way count: a program that leaves them out, or rounds other values in their place, can miss the bound.
Values may be sent and summed in bfloat16 or wider, within the bound.
No kernel may reach another device: no remote copies, remote signals or barrier semaphores. Data moves between devices by JAX's collectives and lax.ppermute only.
A program may use at most 704 MiB of HBM per device.

```python
import jax
import jax.numpy as jnp
from jax import lax

D = 1536
H = 12
KVH = 2
HD = 128
FF = 8960
QKV = 2048
TOK_DEV = 256
NDOCS = 8
LEN = 2048
PACKS = 4
N_BLK = 8


def draw_lengths(key, part):
    key = jax.random.fold_in(key, 11)
    limit = (TOK_DEV - 1) // (NDOCS - 1)
    others_count = NDOCS - 1
    pairs = others_count // 2
    raw = jax.random.randint(key, (PACKS, pairs), 1, limit + 1, dtype=jnp.int32)
    pieces = [raw, (limit + 1 - raw).astype(jnp.int32)]
    if others_count % 2 == 1:
        pieces.append(jnp.ones((PACKS, 1), jnp.int32))
    others = jnp.concatenate(pieces, axis=1).astype(jnp.int32)
    scores = jax.random.randint(jax.random.fold_in(key, 7), (PACKS, others_count), 0, 1 << 20, dtype=jnp.int32)
    scores = scores * others_count + jnp.arange(others_count, dtype=jnp.int32)[None, :]
    order = jnp.argsort(scores, axis=1, stable=True).astype(jnp.int32)
    others = jnp.take_along_axis(others, order, axis=1).astype(jnp.int32)
    long_slot = jax.random.randint(jax.random.fold_in(key, 5), (PACKS, 1), 0, NDOCS, dtype=jnp.int32)
    slots = jnp.arange(NDOCS, dtype=jnp.int32)[None, :]
    is_long = slots == long_slot
    other_index = jnp.clip(slots - (slots > long_slot).astype(jnp.int32), 0, others_count - 1).astype(jnp.int32)
    placed = jnp.take_along_axis(others, other_index, axis=1).astype(jnp.int32)
    others_sum = jnp.sum(others, axis=1, keepdims=True).astype(jnp.int32)
    return jnp.where(is_long, TOK_DEV * N_BLK - others_sum, placed).astype(jnp.int32)


def shard_levels(own_key, dims, shards, smallest, largest):
    factor_of, own = 1.0, jax.random.fold_in(own_key, 6)
    for dim, parts in shards:
        steps = jnp.exp(jax.random.uniform(jax.random.fold_in(own, dim), (parts,), jnp.float32, smallest / len(shards), largest / len(shards)))
        factor_of = factor_of * jnp.repeat(steps, dims[dim] // parts).reshape([-1 if axis == dim else 1 for axis in range(len(dims))])
    return factor_of


def centred(own_key, shape, deviation, reach, shards=(), held_as=jnp.bfloat16):
    factor_of = shard_levels(own_key, shape, shards, -0.22, 0.18) if shards else 1.0
    array = jax.random.normal(own_key, shape, jnp.float32) * deviation * factor_of
    return jnp.minimum(jnp.maximum(array, -reach), reach).astype(held_as)


def setup_inputs(seed: int = 0) -> dict:
    splits = jax.random.split(jax.random.key(seed), 12)
    tokens = centred(splits[0], (PACKS, LEN, D), 1.0, 6.0, ((0, 4), (1, 8)))
    lengths = draw_lengths(jax.random.fold_in(splits[11], 71), 0)
    out_grad = centred(splits[2], (PACKS, LEN, D), 1.0, 6.0, ((0, 4), (1, 8)))
    w_qkv = centred(splits[3], (D, QKV), (D // 2) ** -0.5, 0.21875, ((0, 32),), jnp.float32)
    b_qkv = centred(splits[4], (QKV,), 0.1, 0.6, ((0, 32),), jnp.float32)
    w_out = centred(splits[5], (H * HD, D), (H * HD // 16) ** -0.5, 0.625, ((0, 32),), jnp.float32)
    gain_attn = jnp.clip(1.0 + 0.1 * jax.random.normal(splits[6], (D,), jnp.float32), 0.5, 1.5)
    w_gate = centred(splits[7], (D, FF), D ** -0.5, 0.15625, ((0, 32),), jnp.float32)
    w_up = centred(splits[8], (D, FF), D ** -0.5, 0.15625, ((0, 32),), jnp.float32)
    w_down = centred(splits[9], (FF, D), FF ** -0.5, 0.0625, ((0, 32),), jnp.float32)
    gain_mlp = jnp.clip(1.0 + 0.1 * jax.random.normal(splits[10], (D,), jnp.float32), 0.5, 1.5)
    return dict(tokens=tokens, lengths=lengths, out_grad=out_grad, w_qkv=w_qkv, b_qkv=b_qkv, w_out=w_out, gain_attn=gain_attn, w_gate=w_gate, w_up=w_up, w_down=w_down, gain_mlp=gain_mlp)


@jax.custom_vjp
def low(v):
    return lax.optimization_barrier(v.astype(jnp.bfloat16)).astype(jnp.float32)

@jax.custom_vjp
def low_back(v):
    return v

def low_keep(v):
    return (low(v), None)

def low_pass(kept, grad):
    return (grad,)

def back_keep(v):
    return (v, None)

def back_low(kept, grad):
    return (low(grad),)
low.defvjp(low_keep, low_pass)
low_back.defvjp(back_keep, back_low)

def dense(left, right):
    return jnp.dot(left, right, precision=lax.Precision.HIGHEST)

def rms_norm(values, gain):
    return values * lax.rsqrt(lax.optimization_barrier(jnp.mean(values * values, axis=-1, keepdims=True)) + 1e-06) * gain

def rotate(values, position):
    half = values.shape[-1] // 2
    freq = 10000.0 ** (-2.0 * jnp.arange(half, dtype=jnp.float32) / values.shape[-1])
    angle = position.astype(jnp.float32)[:, None] * freq[None, :]
    cosine = jnp.cos(angle)[:, None, :]
    sine = jnp.sin(angle)[:, None, :]
    first = values[..., :half]
    second = values[..., half:]
    return jnp.concatenate([first * cosine - second * sine, second * cosine + first * sine], axis=-1)

def doc_layout(lengths_row, token_index):
    ends = jnp.cumsum(lengths_row).astype(jnp.int32)
    starts = (ends - lengths_row).astype(jnp.int32)
    inside = (token_index[:, None] >= starts[None, :]) & (token_index[:, None] < ends[None, :])
    numbers = jnp.arange(lengths_row.shape[0], dtype=jnp.int32)
    doc_number = lax.optimization_barrier(jnp.sum(jnp.where(inside, numbers[None, :], 0), axis=1)).astype(jnp.int32)
    begin = lax.optimization_barrier(jnp.sum(jnp.where(inside, starts[None, :], 0), axis=1)).astype(jnp.int32)
    return (doc_number, (token_index - begin).astype(jnp.int32))

def attend(q_scaled, k_rot, v_low, doc_number, token_index):
    length = q_scaled.shape[0]
    block = 512 if length % 512 == 0 else length

    def one_block(start):
        queries = lax.dynamic_slice_in_dim(q_scaled, start, block, 0).reshape(block, KVH, H // KVH, HD)
        query_index = lax.dynamic_slice_in_dim(token_index, start, block, 0)
        query_doc = lax.dynamic_slice_in_dim(doc_number, start, block, 0)
        allowed = (query_doc[:, None] == doc_number[None, :]) & (token_index[None, :] <= query_index[:, None])
        scores = low_back(jnp.einsum('tkgd,ukd->kgtu', queries, k_rot, precision=lax.Precision.HIGHEST))
        masked = jnp.where(allowed, scores, -1e+30)
        row_max = lax.optimization_barrier(jnp.max(masked, axis=-1, keepdims=True))
        weights = jnp.where(allowed, jnp.exp(masked - row_max), 0.0)
        row_total = lax.optimization_barrier(jnp.sum(weights, axis=-1, keepdims=True))
        mixed = jnp.einsum('kgtu,ukd->kgtd', low(weights), v_low, precision=lax.Precision.HIGHEST) / row_total
        return mixed.transpose(2, 0, 1, 3).reshape(block, H * HD)
    starts = jnp.arange(length // block, dtype=jnp.int32) * block
    return lax.map(jax.checkpoint(one_block), starts).reshape(length, H * HD)

def pack_forward(stream, lengths_row, rounded):
    w_qkv, b_qkv, w_out, gain_attn, w_gate, w_up, w_down, gain_mlp = rounded
    token_index = jnp.arange(LEN, dtype=jnp.int32)
    doc_number, position = doc_layout(lengths_row, token_index)
    normed = low(rms_norm(stream, gain_attn))
    projected = low_back(dense(normed, w_qkv) + b_qkv)
    width = H * HD
    query = projected[:, :width].reshape(LEN, H, HD)
    key = projected[:, width:width + KVH * HD].reshape(LEN, KVH, HD)
    value = projected[:, width + KVH * HD:].reshape(LEN, KVH, HD)
    q_scaled = low(rotate(query, position) * HD ** (-0.5))
    k_rot = low(rotate(key, position))
    v_low = low(value)
    mixed = low(low_back(attend(q_scaled, k_rot, v_low, doc_number, token_index)))
    middle = stream + low_back(dense(mixed, w_out))
    hidden = low(rms_norm(middle, gain_mlp))
    gate_proj = low_back(dense(hidden, w_gate))
    up_proj = low_back(dense(hidden, w_up))
    activated = low(jax.nn.silu(gate_proj) * up_proj)
    return middle + dense(activated, w_down)

def reference(tokens, lengths, out_grad, w_qkv, b_qkv, w_out, gain_attn, w_gate, w_up, w_down, gain_mlp):

    def layer(stream, *masters):
        rounded = tuple((low(master) for master in masters))

        def one_pack(pair):
            return pack_forward(pair[0], pair[1], rounded)
        return lax.map(jax.checkpoint(one_pack), (stream, lengths))
    masters = (w_qkv, b_qkv, w_out, gain_attn, w_gate, w_up, w_down, gain_mlp)
    result, pullback = jax.vjp(layer, tokens.astype(jnp.float32), *masters)
    grads = pullback(out_grad.astype(jnp.float32))
    return (result.astype(jnp.bfloat16), grads[0].astype(jnp.bfloat16), grads[1], grads[2], grads[3], grads[4], grads[5], grads[6], grads[7], grads[8])
```

```python
import functools

import jax
import jax.numpy as jnp
from jax import lax
from jax.experimental import pallas as pl
from jax.experimental.pallas import tpu as pltpu
from jax.sharding import PartitionSpec as P

H = 12
KVH = 2
HD = 128
G = H // KVH
NEG = -1e30
BF = jnp.bfloat16
F32 = jnp.float32
VMEM_LIMIT = 56 * 1024 * 1024
BOTH = ("blk", "pack")


def chip_shift(block, by, cyclic=True):
    n = lax.axis_size("blk")
    route = [(i, (i + 2 * by) % n) for i in range(n) if cyclic or 0 <= i + 2 * by < n]
    return lax.ppermute(block, "blk", route)


def core_swap(block):
    n = lax.axis_size("blk")
    return lax.ppermute(block, "blk", [(i, i ^ 1) for i in range(n)])


def gather_line(block):
    chips = lax.axis_size("blk") // 2
    mine = jnp.stack([block] + [chip_shift(block, s) for s in range(1, chips)])
    return jnp.stack([mine, core_swap(mine)], axis=1)


def scatter_line(parts):
    chips = parts.shape[0]
    other = core_swap(parts[:, 1])
    mine = parts[:, 0].astype(F32) + other.astype(F32)
    total = mine[0]
    for s in range(1, chips):
        total = total + chip_shift(mine[s].astype(BF), -s).astype(F32)
    return total


def matmul(left, right):
    return jnp.dot(left, right, preferred_element_type=F32)


def matmul_tn(left, right):
    return lax.dot_general(left, right, (((0,), (0,)), ((), ())), preferred_element_type=F32)


def matmul_nt(left, right):
    return lax.dot_general(left, right, (((1,), (1,)), ((), ())), preferred_element_type=F32)


def rms_norm(values, gain):
    return values * lax.rsqrt(jnp.mean(values * values, axis=-1, keepdims=True) + 1e-06) * gain


def turn(x, cosine, sine):
    return x * cosine + pltpu.roll(x, HD // 2, 1) * sine


def qkv_kernel(xn_ref, w_ref, bias_ref, cos_ref, sin_ref, out_ref):
    step = pl.program_id(0)
    proj = matmul(xn_ref[...], w_ref[...]) + bias_ref[...]
    cosine, sine = cos_ref[...], sin_ref[...]

    @pl.when(step < H // 2)
    def _():
        for i in range(2):
            cut = slice(i * HD, (i + 1) * HD)
            out_ref[:, cut] = (turn(proj[:, cut], cosine, sine) * HD**-0.5).astype(BF)

    @pl.when((step >= H // 2) & (step < (H + KVH) // 2))
    def _():
        for i in range(2):
            cut = slice(i * HD, (i + 1) * HD)
            out_ref[:, cut] = turn(proj[:, cut], cosine, sine).astype(BF)

    @pl.when(step >= (H + KVH) // 2)
    def _():
        out_ref[...] = proj.astype(BF)


def qkv_project(xn, w, bias, cosine, sine):
    rows, depth = xn.shape
    cols = w.shape[1]
    return pl.pallas_call(
        qkv_kernel,
        grid=(cols // 256,),
        in_specs=[
            pl.BlockSpec((rows, depth), lambda i: (0, 0)),
            pl.BlockSpec((depth, 256), lambda i: (0, i)),
            pl.BlockSpec((1, 256), lambda i: (0, i)),
            pl.BlockSpec((rows, HD), lambda i: (0, 0)),
            pl.BlockSpec((rows, HD), lambda i: (0, 0)),
        ],
        out_specs=pl.BlockSpec((rows, 256), lambda i: (0, i)),
        out_shape=jax.ShapeDtypeStruct((rows, cols), BF),
        compiler_params=pltpu.CompilerParams(vmem_limit_bytes=VMEM_LIMIT),
        cost_estimate=pl.CostEstimate(
            flops=2 * rows * depth * cols, bytes_accessed=2 * depth * cols, transcendentals=0
        ),
    )(xn, w, bias, cosine, sine)


def allowed_mask(meta_ref, starts_ref, slot, count):
    rows = starts_ref.shape[1]
    key_index = meta_ref[1 + count + slot] + lax.broadcasted_iota(jnp.int32, (rows, rows), 0)
    query_index = meta_ref[0] + lax.broadcasted_iota(jnp.int32, (rows, rows), 1)
    return (key_index >= starts_ref[...]) & (key_index <= query_index)


def forward_kernel(count, meta_ref, q_ref, starts_ref, k_ref, v_ref, att_ref, lse_ref, m, total, acc):
    slot = pl.program_id(1)

    @pl.when(slot == 0)
    def _():
        m[...] = jnp.full(m.shape, NEG, F32)
        total[...] = jnp.zeros(total.shape, F32)
        acc[...] = jnp.zeros(acc.shape, F32)

    @pl.when(meta_ref[1 + slot] == 1)
    def _():
        allowed = allowed_mask(meta_ref, starts_ref, slot, count)
        keys, values = k_ref[0], v_ref[0]
        for g in range(G):
            scores = matmul_nt(keys, q_ref[:, g * HD : (g + 1) * HD])
            scores = jnp.where(allowed, scores, NEG)
            before = m[g : g + 1, :]
            now = jnp.maximum(before, jnp.max(scores, axis=0, keepdims=True))
            weights = jnp.exp(scores - now)
            fade = jnp.exp(before - now)
            m[g : g + 1, :] = now
            total[g : g + 1, :] = total[g : g + 1, :] * fade + jnp.sum(weights, axis=0, keepdims=True)
            acc[g] = acc[g] * fade + matmul_tn(values, weights.astype(BF))

    @pl.when(slot == count - 1)
    def _():
        for g in range(G):
            att_ref[:, g * HD : (g + 1) * HD] = (acc[g] / total[g : g + 1, :]).T
        lse_ref[0] = m[...] + jnp.log(total[...])


def attention_forward(meta, qkv, starts, kv):
    count, rows = kv.shape[0], kv.shape[1]
    width = G * HD

    def pick(h, j, meta_ref):
        return jnp.where(meta_ref[1 + j] == 1, j, 0)

    return pl.pallas_call(
        functools.partial(forward_kernel, count),
        grid_spec=pltpu.PrefetchScalarGridSpec(
            num_scalar_prefetch=1,
            grid=(KVH, count),
            in_specs=[
                pl.BlockSpec((rows, width), lambda h, j, meta_ref: (0, h)),
                pl.BlockSpec((1, rows), lambda h, j, meta_ref: (0, 0)),
                pl.BlockSpec((1, rows, HD), lambda h, j, meta_ref: (pick(h, j, meta_ref), 0, h)),
                pl.BlockSpec((1, rows, HD), lambda h, j, meta_ref: (pick(h, j, meta_ref), 0, KVH + h)),
            ],
            out_specs=[
                pl.BlockSpec((rows, width), lambda h, j, meta_ref: (0, h)),
                pl.BlockSpec((1, 8, rows), lambda h, j, meta_ref: (h, 0, 0)),
            ],
            scratch_shapes=[
                pltpu.VMEM((8, rows), F32),
                pltpu.VMEM((8, rows), F32),
                pltpu.VMEM((G, HD, rows), F32),
            ],
        ),
        out_shape=[
            jax.ShapeDtypeStruct((rows, H * HD), F32),
            jax.ShapeDtypeStruct((KVH, 8, rows), F32),
        ],
        compiler_params=pltpu.CompilerParams(vmem_limit_bytes=VMEM_LIMIT),
        cost_estimate=pl.CostEstimate(
            flops=4 * rows * rows * count * H * HD,
            bytes_accessed=count * rows * 1024,
            transcendentals=rows * rows * count * H,
        ),
    )(meta, qkv, starts, kv, kv)


def backward_kernel(
    count, meta_ref, q_ref, dout_ref, att_ref, lse_ref, starts_ref, k_ref, v_ref, cos_ref, sin_ref,
    dq_ref, dk_ref, dv_ref, delta, dq_sum,
):
    slot = pl.program_id(1)

    @pl.when(slot == 0)
    def _():
        dq_sum[...] = jnp.zeros(dq_sum.shape, F32)
        for g in range(G):
            cut = slice(g * HD, (g + 1) * HD)
            product = dout_ref[:, cut].astype(F32) * att_ref[:, cut]
            delta[g : g + 1, :] = jnp.sum(product.T, axis=0, keepdims=True)

    @pl.when(meta_ref[1 + slot] == 1)
    def _():
        allowed = allowed_mask(meta_ref, starts_ref, slot, count)
        keys, values = k_ref[0], v_ref[0]
        dk = jnp.zeros(keys.shape, F32)
        dv = jnp.zeros(keys.shape, F32)
        for g in range(G):
            cut = slice(g * HD, (g + 1) * HD)
            query, dout = q_ref[:, cut], dout_ref[:, cut]
            scores = matmul_nt(keys, query)
            weights = jnp.where(allowed, jnp.exp(scores - lse_ref[0, g : g + 1, :]), 0.0)
            dv = dv + matmul(weights.astype(BF), dout)
            slope = matmul_nt(values, dout) - delta[g : g + 1, :]
            dscores = (weights * slope).astype(BF)
            dk = dk + matmul(dscores, query)
            dq_sum[:, cut] = dq_sum[:, cut] + matmul_tn(dscores, keys)
        dk_ref[0] = dk.astype(BF)
        dv_ref[0] = dv.astype(BF)

    @pl.when(meta_ref[1 + slot] == 0)
    def _():
        dk_ref[...] = jnp.zeros(dk_ref.shape, BF)
        dv_ref[...] = jnp.zeros(dv_ref.shape, BF)

    @pl.when(slot == count - 1)
    def _():
        for g in range(G):
            cut = slice(g * HD, (g + 1) * HD)
            back = turn(dq_sum[:, cut] * HD**-0.5, cos_ref[...], -sin_ref[...])
            dq_ref[:, cut] = back.astype(BF)


def attention_backward(meta, qkv, dout, att, lse, starts, kv, cosine, sine):
    count, rows = kv.shape[0], kv.shape[1]
    width = G * HD

    def pick(h, j, meta_ref):
        return jnp.where(meta_ref[1 + j] == 1, j, 0)

    whole = lambda h, j, meta_ref: (0, 0)
    by_head = lambda h, j, meta_ref: (0, h)
    return pl.pallas_call(
        functools.partial(backward_kernel, count),
        grid_spec=pltpu.PrefetchScalarGridSpec(
            num_scalar_prefetch=1,
            grid=(KVH, count),
            in_specs=[
                pl.BlockSpec((rows, width), by_head),
                pl.BlockSpec((rows, width), by_head),
                pl.BlockSpec((rows, width), by_head),
                pl.BlockSpec((1, 8, rows), lambda h, j, meta_ref: (h, 0, 0)),
                pl.BlockSpec((1, rows), whole),
                pl.BlockSpec((1, rows, HD), lambda h, j, meta_ref: (pick(h, j, meta_ref), 0, h)),
                pl.BlockSpec((1, rows, HD), lambda h, j, meta_ref: (pick(h, j, meta_ref), 0, KVH + h)),
                pl.BlockSpec((rows, HD), whole),
                pl.BlockSpec((rows, HD), whole),
            ],
            out_specs=[
                pl.BlockSpec((rows, width), by_head),
                pl.BlockSpec((1, rows, HD), lambda h, j, meta_ref: (j, 0, h)),
                pl.BlockSpec((1, rows, HD), lambda h, j, meta_ref: (j, 0, h)),
            ],
            scratch_shapes=[pltpu.VMEM((8, rows), F32), pltpu.VMEM((rows, width), F32)],
        ),
        out_shape=[
            jax.ShapeDtypeStruct((rows, H * HD), BF),
            jax.ShapeDtypeStruct((count, rows, KVH * HD), BF),
            jax.ShapeDtypeStruct((count, rows, KVH * HD), BF),
        ],
        compiler_params=pltpu.CompilerParams(vmem_limit_bytes=VMEM_LIMIT),
        cost_estimate=pl.CostEstimate(
            flops=10 * rows * rows * count * H * HD,
            bytes_accessed=count * rows * 1024,
            transcendentals=rows * rows * count * H,
        ),
    )(meta, qkv, dout, att, lse, starts, kv, kv, cosine, sine)


def on_device(
    tokens, lengths, out_grad, w_qkv, b_qkv, w_out, gain_attn, w_gate, w_up, w_down, gain_mlp
):
    rows, width = tokens.shape[1:]
    blocks, packs = lax.axis_size("blk"), lax.axis_size("pack")
    chips = blocks // 2
    blk = lax.axis_index("blk")
    chip, core = blk // 2, blk % 2
    depth = w_qkv.shape[0]
    qkv_cols = w_qkv.shape[1]
    ff = w_gate.shape[1] // blocks

    token_index = blk * rows + jnp.arange(rows, dtype=jnp.int32)
    ends = jnp.cumsum(lengths[0])
    doc_starts = ends - lengths[0]
    inside = (token_index[:, None] >= doc_starts[None, :]) & (token_index[:, None] < ends[None, :])
    begin = jnp.sum(jnp.where(inside, doc_starts[None, :], 0), axis=1)
    half = HD // 2
    freq = 10000.0 ** (-2.0 * jnp.arange(half, dtype=F32) / HD)
    angle = (token_index - begin).astype(F32)[:, None] * freq[None, :]
    cosine, sine = jnp.cos(angle), jnp.sin(angle)
    cosine = jnp.concatenate([cosine, cosine], axis=1)
    sine = jnp.concatenate([-sine, sine], axis=1)
    starts = begin[None, :].astype(jnp.int32)

    bias_n, gain_n = b_qkv.shape[0], gain_attn.shape[0]
    vectors = jnp.concatenate([b_qkv, gain_attn, gain_mlp]).astype(BF)
    vectors = jnp.pad(vectors, (0, qkv_cols - vectors.shape[0]))
    spare = jnp.zeros((7, qkv_cols), BF)
    packed = jnp.concatenate([w_qkv.astype(BF), vectors[None], spare])
    packed = lax.all_gather(packed, BOTH, axis=0, tiled=False)
    qkv_full = packed[:, :depth].reshape(width, qkv_cols)
    bias = packed[:, depth, :bias_n].reshape(1, qkv_cols).astype(F32)
    attn_gain = packed[:, depth, bias_n : bias_n + gain_n].reshape(width).astype(F32)
    mlp_gain = packed[:, depth, bias_n + gain_n : bias_n + 2 * gain_n].reshape(width).astype(F32)
    out_full = lax.all_gather(w_out.astype(BF), BOTH, axis=0, tiled=True)

    gate_up = jnp.stack([w_gate, w_up]).astype(BF).reshape(2, depth, blocks, ff)
    gate_up = lax.all_to_all(gate_up.transpose(2, 0, 1, 3), "blk", 0, 0, tiled=True)
    down = lax.all_gather(w_down.astype(BF), "pack", axis=0, tiled=True)
    gate_up = lax.all_gather(gate_up, "pack", axis=0, tiled=False)
    gate_up = gate_up.transpose(2, 1, 0, 3, 4).reshape(2, width, ff)
    gate_w, up_w = gate_up[0], gate_up[1]

    stream = tokens[0].astype(F32)
    normed = rms_norm(stream, attn_gain).astype(BF)
    qkv = qkv_project(normed, qkv_full, bias, cosine, sine)
    own = qkv[:, H * HD :]
    lines = jnp.stack([own] + [chip_shift(own, s, cyclic=False) for s in range(1, chips)])
    kv = jnp.stack([lines, core_swap(lines)], axis=1).reshape(blocks, rows, 2 * KVH * HD)
    back = jnp.arange(chips, dtype=jnp.int32)
    source = jnp.stack([(chip - back) * 2 + core, (chip - back) * 2 + 1 - core], axis=1).reshape(-1)
    valid = ((source >= 0) & (source <= blk)).astype(jnp.int32)
    meta = jnp.concatenate([(blk * rows)[None], valid, source * rows]).astype(jnp.int32)
    att, lse = attention_forward(meta, qkv, starts, kv)
    att_low = att.astype(BF)
    middle = stream + matmul(att_low, out_full)

    grad_top = out_grad[0]
    tops = gather_line(grad_top).reshape(-1, width)
    hidden = rms_norm(middle, mlp_gain).astype(BF)
    hiddens = gather_line(hidden).reshape(-1, width)
    gate = matmul(hiddens, gate_w)
    up = matmul(hiddens, up_w)
    act = (jax.nn.silu(gate) * up).astype(BF)
    partial = matmul(act, down).astype(BF)
    result = middle + scatter_line(partial.reshape(chips, 2, rows, width))

    dact = matmul_nt(tops, down)
    sig = jax.nn.sigmoid(gate)
    dgate = (dact * up * sig * (1 + gate * (1 - sig))).astype(BF)
    dup = (dact * gate * sig).astype(BF)
    dpartial = (matmul_nt(dgate, gate_w) + matmul_nt(dup, up_w)).astype(BF)
    grad_hidden = scatter_line(dpartial.reshape(chips, 2, rows, width))

    grad_down = matmul_tn(act, tops).astype(BF)
    grad_down = lax.psum_scatter(grad_down, "pack", scatter_dimension=0, tiled=True).astype(F32)
    grad_gu = jnp.stack([matmul_tn(hiddens, dgate), matmul_tn(hiddens, dup)]).astype(BF)
    grad_gu = grad_gu.reshape(2, blocks, packs, depth, ff).transpose(2, 1, 0, 3, 4)
    grad_gu = lax.psum_scatter(grad_gu, "pack", scatter_dimension=0, tiled=False)
    grad_gu = lax.all_to_all(grad_gu, "blk", 0, 0, tiled=True)
    grad_gu = grad_gu.transpose(1, 2, 0, 3).reshape(2, depth, blocks * ff).astype(F32)

    _, second_pull = jax.vjp(rms_norm, middle, mlp_gain)
    grad_mid, grad_mlp_gain = second_pull(grad_hidden)
    grad_middle = grad_top.astype(F32) + grad_mid

    middle_low = grad_middle.astype(BF)
    grad_out_w = matmul_tn(att_low, middle_low).astype(BF)
    grad_out_w = lax.psum_scatter(grad_out_w, BOTH, scatter_dimension=0, tiled=True).astype(F32)
    dout = matmul_nt(middle_low, out_full).astype(BF)
    dq, dk, dv = attention_backward(meta, qkv, dout, att, lse, starts, kv, cosine, sine)
    dkv = jnp.concatenate([dk, dv], axis=2).reshape(chips, 2, rows, 2 * KVH * HD)
    mine = dkv[:, 0].astype(F32) + core_swap(dkv[:, 1]).astype(F32)
    pair = mine[0]
    for s in range(1, chips):
        pair = pair + chip_shift(mine[s].astype(BF), -s, cyclic=False).astype(F32)
    dk_own = pair[:, : KVH * HD].reshape(rows, KVH, 2, half)
    swapped = jnp.concatenate([dk_own[:, :, 1:], dk_own[:, :, :1]], axis=2)
    cos4, sin4 = cosine.reshape(rows, 1, 2, half), sine.reshape(rows, 1, 2, half)
    dk_own = (dk_own * cos4 - swapped * sin4).reshape(rows, KVH * HD)
    dproj = jnp.concatenate([dq, dk_own.astype(BF), pair[:, KVH * HD :].astype(BF)], axis=1)

    grad_normed = matmul_nt(dproj, qkv_full)
    _, first_pull = jax.vjp(rms_norm, stream, attn_gain)
    grad_input, grad_attn_gain = first_pull(grad_normed)
    input_grad = (grad_middle + grad_input).astype(BF)
    grad_qkv = matmul_tn(normed, dproj).astype(BF).reshape(blocks * packs, depth, qkv_cols)
    grad_bias = jnp.sum(dproj.astype(F32), axis=0)
    vector_grads = jnp.concatenate(
        [
            grad_bias.reshape(-1, bias_n),
            grad_attn_gain.reshape(-1, gain_n),
            grad_mlp_gain.reshape(-1, gain_n),
        ],
        axis=1,
    ).astype(BF)
    vector_grads = jnp.pad(vector_grads, ((0, 0), (0, qkv_cols - vector_grads.shape[1])))
    spare = jnp.zeros((blocks * packs, 7, qkv_cols), BF)
    attn_grads = jnp.concatenate([grad_qkv, vector_grads[:, None], spare], axis=1)
    attn_grads = lax.psum_scatter(attn_grads, BOTH, scatter_dimension=0, tiled=False).astype(F32)
    tail = attn_grads[depth]
    return (
        result.astype(BF)[None],
        input_grad[None],
        attn_grads[:depth],
        tail[:bias_n],
        grad_out_w,
        tail[bias_n : bias_n + gain_n],
        grad_gu[0],
        grad_gu[1],
        grad_down,
        tail[bias_n + gain_n : bias_n + 2 * gain_n],
    )


def solution(mesh):
    tokens, rows, vector = P("pack", "blk", None), P(BOTH, None), P(BOTH)
    in_specs = (
        tokens, P("pack", None), tokens, rows, vector, rows, vector, rows, rows, rows, vector
    )
    out_specs = (tokens, tokens, rows, vector, rows, vector, rows, rows, rows, vector)
    return jax.shard_map(
        on_device, mesh=mesh, in_specs=in_specs, out_specs=out_specs, check_vma=False
    )
```

```python
import functools

import jax
import jax.numpy as jnp
from jax import lax
from jax.experimental import pallas as pl
from jax.experimental.pallas import tpu as pltpu
from jax.sharding import PartitionSpec as P

H = 12
KVH = 2
HD = 128
G = H // KVH
NEG = -1e30
BF = jnp.bfloat16
F32 = jnp.float32
VMEM_LIMIT = 56 * 1024 * 1024
BOTH = ("blk", "pack")


def chip_shift(block, by, cyclic=True):
    n = lax.axis_size("blk")
    route = [(i, (i + 2 * by) % n) for i in range(n) if cyclic or 0 <= i + 2 * by < n]
    return lax.ppermute(block, "blk", route)


def core_swap(block):
    n = lax.axis_size("blk")
    return lax.ppermute(block, "blk", [(i, i ^ 1) for i in range(n)])


def pack_swap(block, k):
    n = lax.axis_size("pack")
    return lax.ppermute(block, "pack", [(i, i ^ k) for i in range(n)])


def put(buffer, piece, *index):
    piece = piece.reshape((1,) * len(index) + piece.shape)
    zeros = (0,) * (buffer.ndim - len(index))
    return lax.dynamic_update_slice(buffer, piece, tuple(index) + zeros)


def take(array, axis, index):
    return lax.dynamic_index_in_dim(array, index, axis, keepdims=False)


class Place:
    def __init__(self):
        self.blocks, self.packs = lax.axis_size("blk"), lax.axis_size("pack")
        self.chips = self.blocks // 2
        self.blk, self.pack = lax.axis_index("blk"), lax.axis_index("pack")
        self.chip, self.core = self.blk // 2, self.blk % 2

    def chip_at(self, by):
        return lax.rem(self.chip + by + self.chips, self.chips)


def in_core_order(place, mine, other):
    first = jnp.where(place.core == 0, mine, other)
    second = jnp.where(place.core == 0, other, mine)
    return jnp.stack([first, second], axis=1)


def after(value, *before):
    return lax.optimization_barrier((value, before))[0]


def gather_line(block):
    chips = lax.axis_size("blk") // 2
    return jnp.stack([block] + [chip_shift(block, s) for s in range(1, chips)])


def exchange_packs(place, parts):
    got = [take(parts, 0, place.pack)]
    for k in range(1, place.packs):
        got.append(pack_swap(take(parts, 0, place.pack ^ k), k))
    return got


def reduce_line(place, parts):
    other = core_swap(take(parts, 1, 1 - place.core))
    mine = take(parts, 1, place.core).astype(F32) + other.astype(F32)
    line = mine.astype(BF)
    total = take(mine, 0, place.chip)
    for s in range(1, place.chips):
        total = total + chip_shift(take(line, 0, place.chip_at(s)), s).astype(F32)
    return total


def by_columns(matrix, packs):
    return jnp.stack(jnp.split(matrix, packs, axis=1))


def in_pack_order(place, pieces):
    ordered = []
    for q in range(place.packs):
        chosen = pieces[q]
        for p in range(1, place.packs):
            chosen = jnp.where(place.pack == p, pieces[q ^ p], chosen)
        ordered.append(chosen)
    return ordered


def to_shard(place, grad, depth):
    pieces = exchange_packs(place, grad.reshape(place.packs, depth, -1))
    return jnp.concatenate(in_pack_order(place, pieces), axis=1).astype(F32)


def exchange_line(place, parts, beside=()):
    got = jnp.zeros(parts.shape, parts.dtype)
    got = put(got, take(parts, 0, place.chip), place.chip)
    for s in range(1, place.chips):
        got = put(got, chip_shift(take(parts, 0, place.chip_at(s)), s), place.chip_at(-s))
    got = after(got, beside)
    other = core_swap(take(got, 1, 1 - place.core))
    return in_core_order(place, take(got, 1, place.core), other)


def matmul(left, right):
    return jnp.dot(left, right, preferred_element_type=F32)


def matmul_tn(left, right):
    return lax.dot_general(left, right, (((0,), (0,)), ((), ())), preferred_element_type=F32)


def matmul_nt(left, right):
    return lax.dot_general(left, right, (((1,), (1,)), ((), ())), preferred_element_type=F32)


def rms_norm(values, gain):
    return values * lax.rsqrt(jnp.mean(values * values, axis=-1, keepdims=True) + 1e-06) * gain


def turn(x, cosine, sine):
    return x * cosine + pltpu.roll(x, HD // 2, 1) * sine


def qkv_kernel(xn_ref, w_ref, bias_ref, cos_ref, sin_ref, out_ref):
    step = pl.program_id(0)
    proj = matmul(xn_ref[...], w_ref[...]) + bias_ref[...]
    cosine, sine = cos_ref[...], sin_ref[...]

    @pl.when(step < H // 2)
    def _():
        for i in range(2):
            cut = slice(i * HD, (i + 1) * HD)
            out_ref[:, cut] = (turn(proj[:, cut], cosine, sine) * HD**-0.5).astype(BF)

    @pl.when((step >= H // 2) & (step < (H + KVH) // 2))
    def _():
        for i in range(2):
            cut = slice(i * HD, (i + 1) * HD)
            out_ref[:, cut] = turn(proj[:, cut], cosine, sine).astype(BF)

    @pl.when(step >= (H + KVH) // 2)
    def _():
        out_ref[...] = proj.astype(BF)


def qkv_project(xn, w, bias, cosine, sine):
    rows, depth = xn.shape
    cols = w.shape[1]
    return pl.pallas_call(
        qkv_kernel,
        grid=(cols // 256,),
        in_specs=[
            pl.BlockSpec((rows, depth), lambda i: (0, 0)),
            pl.BlockSpec((depth, 256), lambda i: (0, i)),
            pl.BlockSpec((1, 256), lambda i: (0, i)),
            pl.BlockSpec((rows, HD), lambda i: (0, 0)),
            pl.BlockSpec((rows, HD), lambda i: (0, 0)),
        ],
        out_specs=pl.BlockSpec((rows, 256), lambda i: (0, i)),
        out_shape=jax.ShapeDtypeStruct((rows, cols), BF),
        compiler_params=pltpu.CompilerParams(vmem_limit_bytes=VMEM_LIMIT),
        cost_estimate=pl.CostEstimate(
            flops=2 * rows * depth * cols, bytes_accessed=2 * depth * cols, transcendentals=0
        ),
    )(xn, w, bias, cosine, sine)


def allowed_mask(meta_ref, starts_ref, slot, count):
    rows, lanes = starts_ref.shape[1], G * starts_ref.shape[1]
    starts = jnp.concatenate([starts_ref[...]] * G, axis=1)
    key_index = meta_ref[1 + count + slot] + lax.broadcasted_iota(jnp.int32, (rows, lanes), 0)
    query = lax.rem(lax.broadcasted_iota(jnp.int32, (1, lanes), 1), rows)
    return (key_index >= starts) & (key_index <= meta_ref[0] + query)


def stack_heads(target, source_ref):
    rows = source_ref.shape[0]
    for g in range(G):
        target[g * rows : (g + 1) * rows, :] = source_ref[:, g * HD : (g + 1) * HD]


def when_needed(meta_ref, count, work, pieces):
    slot = pl.program_id(1)
    state = meta_ref[1 + slot]
    for core, (k_ref, v_ref) in enumerate(pieces):
        here = slot < count // 2 if core == 0 else slot >= count // 2
        for masked in (True, False):

            @pl.when(here & (state == (1 if masked else 2)))
            def _(k_ref=k_ref, v_ref=v_ref, masked=masked):
                work(k_ref[0], v_ref[0], masked)


def forward_kernel(
    count, meta_ref, q_ref, starts_ref, k0_ref, v0_ref, k1_ref, v1_ref,
    att_ref, low_ref, lse_ref, q, m, total, acc,
):
    slot = pl.program_id(1)
    rows = q_ref.shape[0]

    @pl.when(slot == 0)
    def _():
        stack_heads(q, q_ref)
        m[...] = jnp.full(m.shape, NEG, F32)
        total[...] = jnp.zeros(total.shape, F32)
        acc[...] = jnp.zeros(acc.shape, F32)

    def work(keys, values, masked):
        scores = matmul_nt(keys, q[...])
        if masked:
            scores = jnp.where(allowed_mask(meta_ref, starts_ref, slot, count), scores, NEG)
        before = m[...]
        now = jnp.maximum(before, jnp.max(scores, axis=0, keepdims=True))
        weights = jnp.exp(scores - now)
        fade = jnp.exp(before - now)
        m[...] = now
        total[...] = total[...] * fade + jnp.sum(weights, axis=0, keepdims=True)
        acc[...] = acc[...] * fade + matmul_tn(values, weights.astype(BF))

    when_needed(meta_ref, count, work, ((k0_ref, v0_ref), (k1_ref, v1_ref)))

    @pl.when(slot == count - 1)
    def _():
        out = acc[...] / total[...]
        for g in range(G):
            head = out[:, g * rows : (g + 1) * rows].T
            att_ref[:, g * HD : (g + 1) * HD] = head
            low_ref[:, g * HD : (g + 1) * HD] = head.astype(BF)
        lse_ref[0] = m[...] + jnp.log(total[...])


def kv_specs(count, rows):
    half = count // 2
    specs = []
    for core in range(2):
        for first in (0, KVH):

            def where(h, j, meta_ref, core=core, first=first):
                here = (j < half) if core == 0 else (j >= half)
                index = jnp.where(here & (meta_ref[1 + j] > 0), j - core * half, 0)
                return (index, 0, first + h)

            specs.append(pl.BlockSpec((1, rows, HD), where))
    return specs


def attention_forward(meta, qkv, starts, line, other):
    count, rows = 2 * line.shape[0], line.shape[1]
    width = G * HD
    by_head = lambda h, j, meta_ref: (0, h)
    return pl.pallas_call(
        functools.partial(forward_kernel, count),
        grid_spec=pltpu.PrefetchScalarGridSpec(
            num_scalar_prefetch=1,
            grid=(KVH, count),
            in_specs=[
                pl.BlockSpec((rows, width), by_head),
                pl.BlockSpec((1, rows), lambda h, j, meta_ref: (0, 0)),
            ]
            + kv_specs(count, rows),
            out_specs=[
                pl.BlockSpec((rows, width), by_head),
                pl.BlockSpec((rows, width), by_head),
                pl.BlockSpec((1, 1, G * rows), lambda h, j, meta_ref: (h, 0, 0)),
            ],
            scratch_shapes=[
                pltpu.VMEM((G * rows, HD), BF),
                pltpu.VMEM((1, G * rows), F32),
                pltpu.VMEM((1, G * rows), F32),
                pltpu.VMEM((HD, G * rows), F32),
            ],
        ),
        out_shape=[
            jax.ShapeDtypeStruct((rows, H * HD), F32),
            jax.ShapeDtypeStruct((rows, H * HD), BF),
            jax.ShapeDtypeStruct((KVH, 1, G * rows), F32),
        ],
        compiler_params=pltpu.CompilerParams(vmem_limit_bytes=VMEM_LIMIT),
        cost_estimate=pl.CostEstimate(
            flops=16 * rows * rows * count * H * HD,
            bytes_accessed=count * rows * 1024,
            transcendentals=rows * rows * count * H,
        ),
    )(meta, qkv, starts, line, line, other, other)


def backward_kernel(
    count, meta_ref, q_ref, dout_ref, att_ref, lse_ref, starts_ref, k0_ref, v0_ref, k1_ref, v1_ref,
    cos_ref, sin_ref, dq_ref, dk0_ref, dv0_ref, dk1_ref, dv1_ref, q, dout, delta, dq_sum,
):
    slot = pl.program_id(1)
    rows = q_ref.shape[0]
    half = count // 2

    @pl.when(slot == 0)
    def _():
        stack_heads(q, q_ref)
        stack_heads(dout, dout_ref)
        dq_sum[...] = jnp.zeros(dq_sum.shape, F32)
        for g in range(G):
            cut = slice(g * HD, (g + 1) * HD)
            product = dout_ref[:, cut].astype(F32) * att_ref[:, cut]
            delta[:, g * rows : (g + 1) * rows] = jnp.sum(product.T, axis=0, keepdims=True)

    def work(keys, values, masked):
        weights = jnp.exp(matmul_nt(keys, q[...]) - lse_ref[0])
        if masked:
            weights = jnp.where(allowed_mask(meta_ref, starts_ref, slot, count), weights, 0.0)
        dv = matmul(weights.astype(BF), dout[...]).astype(BF)
        dscores = (weights * (matmul_nt(values, dout[...]) - delta[...])).astype(BF)
        dk = matmul(dscores, q[...]).astype(BF)
        dq_sum[...] = dq_sum[...] + matmul_tn(keys, dscores)

        @pl.when(slot < half)
        def _():
            dk0_ref[0], dv0_ref[0] = dk, dv

        @pl.when(slot >= half)
        def _():
            dk1_ref[0], dv1_ref[0] = dk, dv

    @pl.when((meta_ref[1 + slot] == 0) & (slot < half))
    def _():
        dk0_ref[...] = jnp.zeros(dk0_ref.shape, BF)
        dv0_ref[...] = jnp.zeros(dv0_ref.shape, BF)

    @pl.when((meta_ref[1 + slot] == 0) & (slot >= half))
    def _():
        dk1_ref[...] = jnp.zeros(dk1_ref.shape, BF)
        dv1_ref[...] = jnp.zeros(dv1_ref.shape, BF)

    when_needed(meta_ref, count, work, ((k0_ref, v0_ref), (k1_ref, v1_ref)))

    @pl.when(slot == count - 1)
    def _():
        for g in range(G):
            back = dq_sum[:, g * rows : (g + 1) * rows].T * HD**-0.5
            dq_ref[:, g * HD : (g + 1) * HD] = turn(back, cos_ref[...], -sin_ref[...]).astype(BF)


def attention_backward(meta, qkv, dout, att, lse, starts, line, other, cosine, sine):
    chips, rows = line.shape[:2]
    count = 2 * chips
    width = G * HD
    whole = lambda h, j, meta_ref: (0, 0)
    by_head = lambda h, j, meta_ref: (0, h)
    own = pl.BlockSpec((1, rows, HD), lambda h, j, meta_ref: (jnp.minimum(j, chips - 1), 0, h))
    far = pl.BlockSpec((1, rows, HD), lambda h, j, meta_ref: (jnp.maximum(j - chips, 0), 0, h))
    return pl.pallas_call(
        functools.partial(backward_kernel, count),
        grid_spec=pltpu.PrefetchScalarGridSpec(
            num_scalar_prefetch=1,
            grid=(KVH, count),
            in_specs=[
                pl.BlockSpec((rows, width), by_head),
                pl.BlockSpec((rows, width), by_head),
                pl.BlockSpec((rows, width), by_head),
                pl.BlockSpec((1, 1, G * rows), lambda h, j, meta_ref: (h, 0, 0)),
                pl.BlockSpec((1, rows), whole),
            ]
            + kv_specs(count, rows)
            + [pl.BlockSpec((rows, HD), whole)] * 2,
            out_specs=[pl.BlockSpec((rows, width), by_head), own, own, far, far],
            scratch_shapes=[
                pltpu.VMEM((G * rows, HD), BF),
                pltpu.VMEM((G * rows, HD), BF),
                pltpu.VMEM((1, G * rows), F32),
                pltpu.VMEM((HD, G * rows), F32),
            ],
        ),
        out_shape=[jax.ShapeDtypeStruct((rows, H * HD), BF)]
        + [jax.ShapeDtypeStruct((chips, rows, KVH * HD), BF)] * 4,
        compiler_params=pltpu.CompilerParams(vmem_limit_bytes=VMEM_LIMIT),
        cost_estimate=pl.CostEstimate(
            flops=100 * rows * rows * count * H * HD,
            bytes_accessed=count * rows * 1024,
            transcendentals=rows * rows * count * H,
        ),
    )(meta, qkv, dout, att, lse, starts, line, line, other, other, cosine, sine)


def assemble_kernel(packs, depth, at_ref, *refs):
    *sources, out_ref, sems = refs
    chips = sources[0].shape[0]
    chip, core, pack = at_ref[0], at_ref[1], at_ref[2]
    copies = []
    for n, source in enumerate(sources):
        k, other = n // 2, n % 2
        for s in range(chips):
            place = lax.rem(chip - s + chips, chips) * 2 + (core ^ other)
            start = pl.multiple_of((place * packs + (pack ^ k)) * depth, depth)
            copies.append(
                pltpu.make_async_copy(
                    source.at[s, pl.ds(0, depth)],
                    out_ref.at[pl.ds(start, depth)],
                    sems.at[len(copies)],
                )
            )
    for copy in copies:
        copy.start()
    for copy in copies:
        copy.wait()


def assemble(place, lines, depth):
    chips, _, cols = lines[0].shape
    count = len(lines) * chips
    if depth % 16:
        out = jnp.zeros((count, depth, cols), lines[0].dtype)
        for n, line in enumerate(lines):
            for s in range(chips):
                where = (place.chip_at(-s) * 2 + (place.core ^ (n % 2))) * place.packs
                out = put(out, line[s, :depth], where + (place.pack ^ (n // 2)))
        return out.reshape(count * depth, cols)
    at = jnp.stack([place.chip, place.core, place.pack]).astype(jnp.int32)
    return pl.pallas_call(
        functools.partial(assemble_kernel, place.packs, depth),
        grid_spec=pltpu.PrefetchScalarGridSpec(
            num_scalar_prefetch=1,
            grid=(1,),
            in_specs=[pl.BlockSpec(memory_space=pl.ANY)] * len(lines),
            out_specs=pl.BlockSpec((count * depth, cols), lambda i, at_ref: (0, 0)),
            scratch_shapes=[pltpu.SemaphoreType.DMA((count,))],
        ),
        out_shape=jax.ShapeDtypeStruct((count * depth, cols), lines[0].dtype),
        compiler_params=pltpu.CompilerParams(vmem_limit_bytes=VMEM_LIMIT),
        cost_estimate=pl.CostEstimate(
            flops=0, bytes_accessed=4 * count * depth * cols, transcendentals=0
        ),
    )(at, *lines)


def feed_kernel(
    h0_ref, h1_ref, t0_ref, t1_ref, gate_ref, up_ref, down_ref, *refs
):
    act0_ref, dgate0_ref, dup0_ref, act1_ref, dgate1_ref, dup1_ref, own_ref, other_ref, h, t = refs[-10:]
    rows = h0_ref.shape[1]
    h[:rows], h[rows:] = h0_ref[0], h1_ref[0]
    t[:rows], t[rows:] = t0_ref[0], t1_ref[0]
    gate = matmul(h[...], gate_ref[...])
    up = matmul(h[...], up_ref[...])
    dact = matmul_nt(t[...], down_ref[...])
    sig = 1.0 / (1.0 + jnp.exp(-gate))
    silu = gate * sig
    act = (silu * up).astype(BF)
    dgate = (dact * up * (sig * (1.0 + gate * (1.0 - sig)))).astype(BF)
    dup = (dact * silu).astype(BF)
    act0_ref[0], act1_ref[0] = act[:rows], act[rows:]
    dgate0_ref[0], dgate1_ref[0] = dgate[:rows], dgate[rows:]
    dup0_ref[0], dup1_ref[0] = dup[:rows], dup[rows:]
    part = matmul_nt(dgate, gate_ref[...]) + matmul_nt(dup, up_ref[...])
    own_ref[0] = part[:rows]
    other_ref[0] = part[rows:].astype(BF)


def feed(hs, ts, gate_w, up_w, down):
    count, rows, width = hs[0].shape
    ff = gate_w.shape[1]
    entry = lambda i: (i, 0, 0)
    whole = lambda i: (0, 0)
    once = pl.Buffered(1)
    tokens = pl.BlockSpec((1, rows, width), entry)
    column = pl.BlockSpec((1, rows, ff), entry)
    return pl.pallas_call(
        feed_kernel,
        grid=(count,),
        in_specs=[tokens] * 4
        + [
            pl.BlockSpec((width, ff), whole, pipeline_mode=once),
            pl.BlockSpec((width, ff), whole, pipeline_mode=once),
            pl.BlockSpec((ff, width), whole, pipeline_mode=once),
        ],
        out_specs=[column] * 6 + [tokens] * 2,
        out_shape=[jax.ShapeDtypeStruct((count, rows, ff), BF)] * 6
        + [
            jax.ShapeDtypeStruct((count, rows, width), F32),
            jax.ShapeDtypeStruct((count, rows, width), BF),
        ],
        scratch_shapes=[pltpu.VMEM((2 * rows, width), BF)] * 2,
        compiler_params=pltpu.CompilerParams(vmem_limit_bytes=VMEM_LIMIT),
        cost_estimate=pl.CostEstimate(
            flops=25 * count * rows * width * ff,
            bytes_accessed=6 * width * ff,
            transcendentals=2 * count * rows * ff,
        ),
    )(*hs, *ts, gate_w, up_w, down)


def grads_kernel(packs, n, *refs):
    *refs, out_ref = refs
    _, near, _, depth, ff = out_ref.shape
    for i in range(2):
        grad = sum(matmul_tn(refs[j][...], refs[n + i * n + j][...]) for j in range(n))
        grad = grad.astype(BF).reshape(near, packs, depth, ff)
        for p in range(packs):
            out_ref[p, :, i] = grad[:, p]


def gate_up_grads(blocks, packs, depth, ff, hs, dgates, dups):
    width = hs[0].shape[1]
    tile = width // 4
    if depth % 16 or tile % (packs * depth):
        grads = [sum(matmul_tn(h, d) for h, d in zip(hs, ds)).astype(BF) for ds in (dgates, dups)]
        return jnp.stack(grads).reshape(2, blocks, packs, depth, ff).transpose(2, 1, 0, 3, 4)
    near = tile // (packs * depth)
    columns = [pl.BlockSpec((h.shape[0], tile), lambda j: (0, j)) for h in hs]
    once = pl.Buffered(1)
    kept = [pl.BlockSpec(d.shape, lambda j: (0, 0), pipeline_mode=once) for d in dgates + dups]
    rows = sum(h.shape[0] for h in hs)
    return pl.pallas_call(
        functools.partial(grads_kernel, packs, len(hs)),
        grid=(4,),
        in_specs=columns + kept,
        out_specs=pl.BlockSpec((packs, near, 2, depth, ff), lambda j: (0, j, 0, 0, 0)),
        out_shape=jax.ShapeDtypeStruct((packs, blocks, 2, depth, ff), BF),
        compiler_params=pltpu.CompilerParams(vmem_limit_bytes=VMEM_LIMIT),
        cost_estimate=pl.CostEstimate(
            flops=7 * rows * width * ff, bytes_accessed=6 * rows * ff, transcendentals=0
        ),
    )(*hs, *dgates, *dups)


def on_device(
    tokens, lengths, out_grad, w_qkv, b_qkv, w_out, gain_attn, w_gate, w_up, w_down, gain_mlp
):
    rows, width = tokens.shape[1:]
    place = Place()
    blocks, packs, chips = place.blocks, place.packs, place.chips
    blk, chip, core = place.blk, place.chip, place.core
    depth = w_qkv.shape[0]
    qkv_cols = w_qkv.shape[1]
    ff = w_gate.shape[1] // blocks
    q_cols = H * HD

    token_index = blk * rows + jnp.arange(rows, dtype=jnp.int32)
    ends = jnp.cumsum(lengths[0])
    doc_starts = ends - lengths[0]
    inside = (token_index[:, None] >= doc_starts[None, :]) & (token_index[:, None] < ends[None, :])
    begin = jnp.sum(jnp.where(inside, doc_starts[None, :], 0), axis=1)
    half = HD // 2
    freq = 10000.0 ** (-2.0 * jnp.arange(half, dtype=F32) / HD)
    angle = (token_index - begin).astype(F32)[:, None] * freq[None, :]
    cosine, sine = jnp.cos(angle), jnp.sin(angle)
    cosine = jnp.concatenate([cosine, cosine], axis=1)
    sine = jnp.concatenate([-sine, sine], axis=1)
    starts = begin[None, :].astype(jnp.int32)

    bias_n, gain_n = b_qkv.shape[0], gain_attn.shape[0]
    shard = blk * packs + place.pack

    def placed(vector):
        row = jnp.zeros((qkv_cols,), BF)
        return lax.dynamic_update_slice(row, vector.astype(BF), (shard * vector.shape[0],))

    spare = jnp.stack([placed(b_qkv), placed(gain_attn), placed(gain_mlp)])
    spare = jnp.pad(spare, ((0, 5), (0, 0)))
    line = gather_line(jnp.concatenate([w_qkv.astype(BF), spare]))
    grad_top = out_grad[0]
    gate_up = jnp.stack([w_gate, w_up]).astype(BF).reshape(2, depth, chips, 2, ff)
    gate_up = after(gate_up.transpose(2, 3, 0, 1, 4), line)
    lines = [line] + [pack_swap(line, k) for k in range(1, packs)]
    lines = [piece for line in lines for piece in (line, core_swap(after(line, lines[1])))]
    gate_up = exchange_line(place, gate_up, lines).reshape(blocks, 2, depth, ff)
    vectors = sum(jnp.sum(piece[:, depth:].astype(F32), axis=0) for piece in lines)
    bias = vectors[:1]
    attn_gain, mlp_gain = vectors[1, :width], vectors[2, :width]
    out_line = gather_line(after(w_out.astype(BF), gate_up))
    qkv_full = assemble(place, lines, depth)

    down = lax.all_gather(after(w_down, lines[2]).astype(BF), "pack", axis=0, tiled=True)
    out_lines = [out_line] + [pack_swap(out_line, k) for k in range(1, packs)]

    def whole(part):
        part = lax.all_gather(part.reshape(blocks * depth, ff), "pack", axis=0, tiled=True)
        part = part.reshape(packs, blocks, depth, ff).transpose(1, 0, 2, 3)
        return part.reshape(width, ff)

    gate_w, up_w = whole(gate_up[:, 0]), whole(gate_up[:, 1])

    stream = tokens[0].astype(F32)
    normed = rms_norm(stream, attn_gain).astype(BF)
    qkv = qkv_project(normed, qkv_full, bias, cosine, sine)
    own = qkv[:, q_cols:]
    kv_line = jnp.stack([own] + [chip_shift(own, s, cyclic=False) for s in range(1, chips)])
    top = after(out_grad[0], gate_up)
    t = {0: grad_top, 1: chip_shift(top, 1)}
    if chips > 2:
        t[chips - 1] = chip_shift(top, -1)
    kv_other = core_swap(after(kv_line, out_lines, t[1]))
    back = jnp.arange(chips, dtype=jnp.int32)
    source = jnp.concatenate([(chip - back) * 2 + core, (chip - back) * 2 + 1 - core])
    valid = ((source >= 0) & (source <= blk)).astype(jnp.int32)
    clear = ((source < blk) & (source * rows >= jnp.max(begin))).astype(jnp.int32)
    meta = jnp.concatenate([(blk * rows)[None], valid * (1 + clear), source * rows])
    meta = meta.astype(jnp.int32)
    att, att_low, lse = attention_forward(meta, qkv, starts, kv_line, kv_other)
    out_lines = after(out_lines, att_low)
    out_lines = [piece for line in out_lines for piece in (line, core_swap(line))]
    out_full = assemble(place, out_lines, depth)
    att_low = after(att_low, t[chips - 1])
    middle = stream + matmul(att_low, out_full)

    hidden = rms_norm(middle, mlp_gain).astype(BF)

    normed_all = lax.all_gather(after(normed, up_w, down), "pack", axis=0, tiled=True)
    att_all = lax.all_gather(after(att_low, up_w, down), "pack", axis=0, tiled=True)

    def both(blocks):
        line = jnp.stack(blocks)
        return line, core_swap(line)

    def pass_back(parts):
        parts = dict(parts)
        for s in reversed(range(2, chips - 1)):
            parts[s - 1] = parts[s - 1] + chip_shift(parts[s].astype(BF), -1).astype(F32)
        return parts

    def give_back(parts):
        total = parts[0] + chip_shift(parts[1].astype(BF), -1).astype(F32)
        if chips > 2:
            total = total + chip_shift(parts[chips - 1].astype(BF), 1).astype(F32)
        return total

    h = {0: hidden, 1: chip_shift(hidden, 1)}
    if chips > 2:
        h[chips - 1] = chip_shift(hidden, -1)
    for s in range(2, chips - 1):
        h[s], t[s] = chip_shift(h[s - 1], 1), chip_shift(t[s - 1], 1)
    h[0], h[chips - 1] = after((h[0], h[chips - 1]), h[chips - 1])
    h[1] = after(h[1], h[chips - 1])
    first, second = (list(range(chips - 2, 0, -1)), [chips - 1, 0]) if chips > 2 else ([1, 0], [])
    hs, ts, fed, partials = [], [], [], {}
    for part in (first, second):
        if not part:
            continue
        h_pair, t_pair = both([h[s] for s in part]), both([t[s] for s in part])
        if partials:
            h_pair = after(h_pair, other)
        *kept, mine, other = feed(h_pair, t_pair, gate_w, up_w, down)
        mine = mine + core_swap(other).astype(F32)
        partials.update({s: mine[i] for i, s in enumerate(part)})
        flat = lambda arrays: [one.reshape(len(part) * rows, -1) for one in arrays]
        hs, ts = hs + flat(h_pair), ts + flat(t_pair)
        fed.append(flat(kept))
    acts, dgates, dups = ([one for kept in fed for one in kept[i::3]] for i in range(3))
    partials = pass_back(partials)
    hs = after(hs, partials)
    grad_hidden = give_back(partials)

    grad_gu = gate_up_grads(blocks, packs, depth, ff, hs, dgates, dups)
    out_parts, outs = [matmul(act, down) for act in after(acts, grad_gu)], {}
    for i, part in enumerate((first, second)):
        if part:
            other = core_swap(out_parts[2 * i + 1].astype(BF))
            mine = (out_parts[2 * i] + other.astype(F32)).reshape(len(part), rows, width)
            outs.update({s: mine[n] for n, s in enumerate(part)})
    grad_hidden = after(grad_hidden, grad_gu)

    grad_gu = after(grad_gu, normed_all, att_all).reshape(packs * blocks * 2 * depth, ff)
    grad_gu = lax.psum_scatter(grad_gu, "pack", scatter_dimension=0, tiled=True)
    gu_here = exchange_line(place, grad_gu.reshape(chips, 2, 2, depth, ff))

    _, second_pull = jax.vjp(rms_norm, middle, mlp_gain)
    grad_mid, grad_mlp_gain = second_pull(grad_hidden)
    grad_middle = grad_top.astype(F32) + grad_mid

    middle_low = grad_middle.astype(BF)

    dout = matmul_nt(middle_low, out_full).astype(BF).reshape(rows, q_cols)
    dout, outs = after((dout, outs), dout, outs)
    outs = pass_back(outs)
    if chips > 2:
        outs[chips - 1] = chip_shift(outs[chips - 1].astype(BF), 1)
    dq, dk0, dv0, dk1, dv1 = attention_backward(
        meta, qkv, dout, att, lse, starts, kv_line, kv_other, cosine, sine
    )
    dk1, dv1, outs = after((dk1, dv1, outs), outs)
    result = middle + outs[0] + chip_shift(outs[1].astype(BF), -1).astype(F32)
    if chips > 2:
        result = result + outs[chips - 1].astype(F32)
    result = result.astype(BF)
    other = core_swap(jnp.concatenate([dk1, dv1], axis=2))
    mine = jnp.concatenate([dk0, dv0], axis=2).astype(F32) + other.astype(F32)
    sent = [by_columns(middle_low, packs), by_columns(after(dq, mine), packs)]
    got = exchange_packs(place, jnp.concatenate(sent, axis=2))
    got = jnp.concatenate(in_pack_order(place, got))
    part = width // packs
    parts = [matmul_tn(att_all, got[:, :part]), matmul_tn(normed_all, got[:, part:])]
    parts = jnp.concatenate(parts, axis=1).astype(BF)
    acts, ts = after((acts, ts), parts)
    pair = mine[0]
    for s in range(1, chips):
        pair = pair + chip_shift(mine[s].astype(BF), -s, cyclic=False).astype(F32)
    turned = []
    for j in range(KVH):
        one = pair[:, j * HD : (j + 1) * HD]
        swapped = jnp.concatenate([one[:, half:], one[:, :half]], axis=1)
        turned.append(one * cosine - swapped * sine)
    dkv = jnp.concatenate(turned + [pair[:, KVH * HD :]], axis=1).astype(BF)
    parts = reduce_line(place, parts.reshape(chips, 2, packs * depth, -1)).astype(BF)
    parts = after(parts, dkv, result)
    got = exchange_packs(place, parts.reshape(packs, depth, -1))
    got = in_pack_order(place, got)
    grad_out_w = jnp.concatenate([piece[:, :part] for piece in got], axis=1).astype(F32)
    grad_q = jnp.concatenate([piece[:, part:] for piece in got], axis=1).astype(F32)
    grad_down = sum(matmul_tn(act, top) for act, top in zip(acts, ts)).astype(BF)
    grad_down = lax.psum_scatter(grad_down, "pack", scatter_dimension=0, tiled=True).astype(F32)
    grad_gu = gu_here.reshape(blocks, 2, depth, ff).transpose(1, 2, 0, 3).reshape(2, depth, -1)
    grad_gate_w, grad_up_w = grad_gu[0].astype(F32), grad_gu[1].astype(F32)
    dkv = after(dkv, gu_here)
    dproj = jnp.concatenate([dq, dkv], axis=1)

    grad_normed = matmul_nt(dproj, qkv_full)
    _, first_pull = jax.vjp(rms_norm, stream, attn_gain)
    grad_input, grad_attn_gain = first_pull(grad_normed)
    input_grad = (grad_middle + grad_input).astype(BF)
    grad_bias = jnp.sum(dproj.astype(F32), axis=0)
    vector_grads = jnp.concatenate(
        [
            grad_bias.reshape(-1, bias_n),
            grad_attn_gain.reshape(-1, gain_n),
            grad_mlp_gain.reshape(-1, gain_n),
        ],
        axis=1,
    ).astype(BF)
    part = (qkv_cols - q_cols) // packs
    lines = -(-vector_grads.shape[1] // part)
    lines += -(blocks * lines) % 16 // blocks
    vector_grads = jnp.pad(vector_grads, ((0, 0), (0, lines * part - vector_grads.shape[1])))
    vector_grads = vector_grads.reshape(blocks, packs, lines, part).transpose(1, 0, 2, 3)
    vector_grads = vector_grads.reshape(packs, blocks * lines, part)
    got = exchange_packs(place, jnp.concatenate([by_columns(dkv, packs), vector_grads], axis=1))
    kv_all = jnp.concatenate(in_pack_order(place, [piece[:rows] for piece in got]))
    grad_kv = matmul_tn(normed_all, kv_all).astype(BF)
    vector_sum = sum(piece[rows:].astype(F32) for piece in got).astype(BF)
    grad_kv = jnp.concatenate(
        [grad_kv.reshape(blocks, packs * depth, part), vector_sum.reshape(blocks, lines, part)],
        axis=1,
    )
    grad_kv = reduce_line(place, grad_kv.reshape(chips, 2, -1, part))
    tail = grad_kv[packs * depth :].reshape(-1)
    grad_kv = to_shard(place, grad_kv[: packs * depth].astype(BF), depth)
    return (
        result[None],
        input_grad[None],
        jnp.concatenate([grad_q, grad_kv], axis=1),
        tail[:bias_n],
        grad_out_w,
        tail[bias_n : bias_n + gain_n],
        grad_gate_w,
        grad_up_w,
        grad_down,
        tail[bias_n + gain_n : bias_n + 2 * gain_n],
    )


def solution(mesh):
    tokens, rows, vector = P("pack", "blk", None), P(BOTH, None), P(BOTH)
    in_specs = (
        tokens, P("pack", None), tokens, rows, vector, rows, vector, rows, rows, rows, vector
    )
    out_specs = (tokens, tokens, rows, vector, rows, vector, rows, rows, rows, vector)
    return jax.shard_map(
        on_device, mesh=mesh, in_specs=in_specs, out_specs=out_specs, check_vma=False
    )
```

```python
import functools

import jax
import jax.numpy as jnp
from jax import lax
from jax.experimental import pallas as pl
from jax.experimental.pallas import tpu as pltpu
from jax.sharding import PartitionSpec as P

H = 12
KVH = 2
HD = 128
G = H // KVH
NEG = -1e30
BF = jnp.bfloat16
F32 = jnp.float32
VMEM_LIMIT = 56 * 1024 * 1024
BOTH = ("blk", "pack")


def chip_shift(block, by, cyclic=True):
    n = lax.axis_size("blk")
    route = [(i, (i + 2 * by) % n) for i in range(n) if cyclic or 0 <= i + 2 * by < n]
    return lax.ppermute(block, "blk", route)


def core_swap(block):
    n = lax.axis_size("blk")
    return lax.ppermute(block, "blk", [(i, i ^ 1) for i in range(n)])


def pack_swap(block, k):
    n = lax.axis_size("pack")
    return lax.ppermute(block, "pack", [(i, i ^ k) for i in range(n)])


def put(buffer, piece, *index):
    piece = piece.reshape((1,) * len(index) + piece.shape)
    zeros = (0,) * (buffer.ndim - len(index))
    return lax.dynamic_update_slice(buffer, piece, tuple(index) + zeros)


def take(array, axis, index):
    return lax.dynamic_index_in_dim(array, index, axis, keepdims=False)


class Place:
    def __init__(self):
        self.blocks, self.packs = lax.axis_size("blk"), lax.axis_size("pack")
        self.chips = self.blocks // 2
        self.blk, self.pack = lax.axis_index("blk"), lax.axis_index("pack")
        self.chip, self.core = self.blk // 2, self.blk % 2

    def chip_at(self, by):
        return lax.rem(self.chip + by + self.chips, self.chips)


def in_core_order(place, mine, other):
    first = jnp.where(place.core == 0, mine, other)
    second = jnp.where(place.core == 0, other, mine)
    return jnp.stack([first, second], axis=1)


def after(value, *before):
    return lax.optimization_barrier((value, before))[0]


def gather_line(block):
    chips = lax.axis_size("blk") // 2
    return jnp.stack([block] + [chip_shift(block, s) for s in range(1, chips)])


def exchange_packs(place, parts):
    got = [take(parts, 0, place.pack)]
    for k in range(1, place.packs):
        got.append(pack_swap(take(parts, 0, place.pack ^ k), k))
    return got


def reduce_line(place, parts, before=()):
    other = core_swap(take(parts, 1, 1 - place.core))
    mine = after(take(parts, 1, place.core).astype(F32) + other.astype(F32), before)
    line = mine.astype(BF)
    total = take(mine, 0, place.chip)
    for s in range(1, place.chips):
        total = total + chip_shift(take(line, 0, place.chip_at(s)), s).astype(F32)
    return total


def by_columns(matrix, packs):
    return jnp.stack(jnp.split(matrix, packs, axis=1))


def in_pack_order(place, pieces):
    ordered = []
    for q in range(place.packs):
        chosen = pieces[q]
        for p in range(1, place.packs):
            chosen = jnp.where(place.pack == p, pieces[q ^ p], chosen)
        ordered.append(chosen)
    return ordered


def to_shard(place, grad, depth):
    pieces = exchange_packs(place, grad.reshape(place.packs, depth, -1))
    return jnp.concatenate(in_pack_order(place, pieces), axis=1).astype(F32)


def exchange_chips(place, parts):
    got = jnp.zeros(parts.shape, parts.dtype)
    got = put(got, take(parts, 0, place.chip), place.chip)
    for s in range(1, place.chips):
        got = put(got, chip_shift(take(parts, 0, place.chip_at(s)), s), place.chip_at(-s))
    return got


def exchange_cores(place, got):
    other = core_swap(take(got, 1, 1 - place.core))
    return in_core_order(place, take(got, 1, place.core), other)


def matmul(left, right):
    return jnp.dot(left, right, preferred_element_type=F32)


def matmul_tn(left, right):
    return lax.dot_general(left, right, (((0,), (0,)), ((), ())), preferred_element_type=F32)


def matmul_nt(left, right):
    return lax.dot_general(left, right, (((1,), (1,)), ((), ())), preferred_element_type=F32)


def rms_norm(values, gain):
    return values * lax.rsqrt(jnp.mean(values * values, axis=-1, keepdims=True) + 1e-06) * gain


def turn(x, cosine, sine):
    return x * cosine + pltpu.roll(x, HD // 2, 1) * sine


def qkv_kernel(xn_ref, w_ref, bias_ref, cos_ref, sin_ref, out_ref):
    step = pl.program_id(0)
    proj = matmul(xn_ref[...], w_ref[...]) + bias_ref[...]
    cosine, sine = cos_ref[...], sin_ref[...]

    @pl.when(step < H // 2)
    def _():
        for i in range(2):
            cut = slice(i * HD, (i + 1) * HD)
            out_ref[:, cut] = (turn(proj[:, cut], cosine, sine) * HD**-0.5).astype(BF)

    @pl.when((step >= H // 2) & (step < (H + KVH) // 2))
    def _():
        for i in range(2):
            cut = slice(i * HD, (i + 1) * HD)
            out_ref[:, cut] = turn(proj[:, cut], cosine, sine).astype(BF)

    @pl.when(step >= (H + KVH) // 2)
    def _():
        out_ref[...] = proj.astype(BF)


def qkv_project(xn, w, bias, cosine, sine):
    rows, depth = xn.shape
    cols = w.shape[1]
    return pl.pallas_call(
        qkv_kernel,
        grid=(cols // 256,),
        in_specs=[
            pl.BlockSpec((rows, depth), lambda i: (0, 0)),
            pl.BlockSpec((depth, 256), lambda i: (0, i)),
            pl.BlockSpec((1, 256), lambda i: (0, i)),
            pl.BlockSpec((rows, HD), lambda i: (0, 0)),
            pl.BlockSpec((rows, HD), lambda i: (0, 0)),
        ],
        out_specs=pl.BlockSpec((rows, 256), lambda i: (0, i)),
        out_shape=jax.ShapeDtypeStruct((rows, cols), BF),
        compiler_params=pltpu.CompilerParams(vmem_limit_bytes=VMEM_LIMIT),
        cost_estimate=pl.CostEstimate(
            flops=2 * rows * depth * cols, bytes_accessed=2 * depth * cols, transcendentals=0
        ),
    )(xn, w, bias, cosine, sine)


def allowed_mask(meta_ref, starts_ref, slot, count):
    rows, lanes = starts_ref.shape[1], G * starts_ref.shape[1]
    starts = jnp.concatenate([starts_ref[...]] * G, axis=1)
    key_index = meta_ref[1 + count + slot] + lax.broadcasted_iota(jnp.int32, (rows, lanes), 0)
    query = lax.rem(lax.broadcasted_iota(jnp.int32, (1, lanes), 1), rows)
    return (key_index >= starts) & (key_index <= meta_ref[0] + query)


def stack_heads(target, source_ref):
    rows = source_ref.shape[0]
    for g in range(G):
        target[g * rows : (g + 1) * rows, :] = source_ref[:, g * HD : (g + 1) * HD]


def when_needed(meta_ref, count, work, pieces):
    slot = pl.program_id(1)
    state = meta_ref[1 + slot]
    for core, (k_ref, v_ref) in enumerate(pieces):
        here = slot < count // 2 if core == 0 else slot >= count // 2
        for masked in (True, False):

            @pl.when(here & (state == (1 if masked else 2)))
            def _(k_ref=k_ref, v_ref=v_ref, masked=masked):
                work(k_ref[0], v_ref[0], masked)


def forward_kernel(
    count, meta_ref, q_ref, starts_ref, k0_ref, v0_ref, k1_ref, v1_ref,
    att_ref, low_ref, lse_ref, q, m, total, acc,
):
    slot = pl.program_id(1)
    rows = q_ref.shape[0]

    @pl.when(slot == 0)
    def _():
        stack_heads(q, q_ref)
        m[...] = jnp.full(m.shape, NEG, F32)
        total[...] = jnp.zeros(total.shape, F32)
        acc[...] = jnp.zeros(acc.shape, F32)

    def work(keys, values, masked):
        scores = matmul_nt(keys, q[...])
        if masked:
            scores = jnp.where(allowed_mask(meta_ref, starts_ref, slot, count), scores, NEG)
        before = m[...]
        now = jnp.maximum(before, jnp.max(scores, axis=0, keepdims=True))
        weights = jnp.exp(scores - now)
        fade = jnp.exp(before - now)
        m[...] = now
        total[...] = total[...] * fade + jnp.sum(weights, axis=0, keepdims=True)
        acc[...] = acc[...] * fade + matmul_tn(values, weights.astype(BF))

    when_needed(meta_ref, count, work, ((k0_ref, v0_ref), (k1_ref, v1_ref)))

    @pl.when(slot == count - 1)
    def _():
        out = acc[...] / total[...]
        for g in range(G):
            head = out[:, g * rows : (g + 1) * rows].T
            att_ref[:, g * HD : (g + 1) * HD] = head
            low_ref[:, g * HD : (g + 1) * HD] = head.astype(BF)
        lse_ref[0] = m[...] + jnp.log(total[...])


def kv_specs(count, rows):
    half = count // 2
    specs = []
    for core in range(2):
        for first in (0, KVH):

            def where(h, j, meta_ref, core=core, first=first):
                here = (j < half) if core == 0 else (j >= half)
                index = jnp.where(here & (meta_ref[1 + j] > 0), j - core * half, 0)
                return (index, 0, first + h)

            specs.append(pl.BlockSpec((1, rows, HD), where))
    return specs


def attention_forward(meta, qkv, starts, line, other):
    count, rows = 2 * line.shape[0], line.shape[1]
    width = G * HD
    by_head = lambda h, j, meta_ref: (0, h)
    return pl.pallas_call(
        functools.partial(forward_kernel, count),
        grid_spec=pltpu.PrefetchScalarGridSpec(
            num_scalar_prefetch=1,
            grid=(KVH, count),
            in_specs=[
                pl.BlockSpec((rows, width), by_head),
                pl.BlockSpec((1, rows), lambda h, j, meta_ref: (0, 0)),
            ]
            + kv_specs(count, rows),
            out_specs=[
                pl.BlockSpec((rows, width), by_head),
                pl.BlockSpec((rows, width), by_head),
                pl.BlockSpec((1, 1, G * rows), lambda h, j, meta_ref: (h, 0, 0)),
            ],
            scratch_shapes=[
                pltpu.VMEM((G * rows, HD), BF),
                pltpu.VMEM((1, G * rows), F32),
                pltpu.VMEM((1, G * rows), F32),
                pltpu.VMEM((HD, G * rows), F32),
            ],
        ),
        out_shape=[
            jax.ShapeDtypeStruct((rows, H * HD), F32),
            jax.ShapeDtypeStruct((rows, H * HD), BF),
            jax.ShapeDtypeStruct((KVH, 1, G * rows), F32),
        ],
        compiler_params=pltpu.CompilerParams(vmem_limit_bytes=VMEM_LIMIT),
        cost_estimate=pl.CostEstimate(
            flops=16 * rows * rows * count * H * HD,
            bytes_accessed=count * rows * 1024,
            transcendentals=rows * rows * count * H,
        ),
    )(meta, qkv, starts, line, line, other, other)


def backward_kernel(
    count, meta_ref, q_ref, dout_ref, att_ref, lse_ref, starts_ref, k0_ref, v0_ref, k1_ref, v1_ref,
    cos_ref, sin_ref, dq_ref, dk0_ref, dv0_ref, dk1_ref, dv1_ref, q, dout, delta, dq_sum,
):
    slot = pl.program_id(1)
    rows = q_ref.shape[0]
    half = count // 2

    @pl.when(slot == 0)
    def _():
        stack_heads(q, q_ref)
        stack_heads(dout, dout_ref)
        dq_sum[...] = jnp.zeros(dq_sum.shape, F32)
        for g in range(G):
            cut = slice(g * HD, (g + 1) * HD)
            product = dout_ref[:, cut].astype(F32) * att_ref[:, cut]
            delta[:, g * rows : (g + 1) * rows] = jnp.sum(product.T, axis=0, keepdims=True)

    def work(keys, values, masked):
        weights = jnp.exp(matmul_nt(keys, q[...]) - lse_ref[0])
        if masked:
            weights = jnp.where(allowed_mask(meta_ref, starts_ref, slot, count), weights, 0.0)
        dv = matmul(weights.astype(BF), dout[...]).astype(BF)
        dscores = (weights * (matmul_nt(values, dout[...]) - delta[...])).astype(BF)
        dk = matmul(dscores, q[...]).astype(BF)
        dq_sum[...] = dq_sum[...] + matmul_tn(keys, dscores)

        @pl.when(slot < half)
        def _():
            dk0_ref[0], dv0_ref[0] = dk, dv

        @pl.when(slot >= half)
        def _():
            dk1_ref[0], dv1_ref[0] = dk, dv

    @pl.when((meta_ref[1 + slot] == 0) & (slot < half))
    def _():
        dk0_ref[...] = jnp.zeros(dk0_ref.shape, BF)
        dv0_ref[...] = jnp.zeros(dv0_ref.shape, BF)

    @pl.when((meta_ref[1 + slot] == 0) & (slot >= half))
    def _():
        dk1_ref[...] = jnp.zeros(dk1_ref.shape, BF)
        dv1_ref[...] = jnp.zeros(dv1_ref.shape, BF)

    when_needed(meta_ref, count, work, ((k0_ref, v0_ref), (k1_ref, v1_ref)))

    @pl.when(slot == count - 1)
    def _():
        for g in range(G):
            back = dq_sum[:, g * rows : (g + 1) * rows].T * HD**-0.5
            dq_ref[:, g * HD : (g + 1) * HD] = turn(back, cos_ref[...], -sin_ref[...]).astype(BF)


def attention_backward(meta, qkv, dout, att, lse, starts, line, other, cosine, sine):
    chips, rows = line.shape[:2]
    count = 2 * chips
    width = G * HD
    whole = lambda h, j, meta_ref: (0, 0)
    by_head = lambda h, j, meta_ref: (0, h)
    own = pl.BlockSpec((1, rows, HD), lambda h, j, meta_ref: (jnp.minimum(j, chips - 1), 0, h))
    far = pl.BlockSpec((1, rows, HD), lambda h, j, meta_ref: (jnp.maximum(j - chips, 0), 0, h))
    return pl.pallas_call(
        functools.partial(backward_kernel, count),
        grid_spec=pltpu.PrefetchScalarGridSpec(
            num_scalar_prefetch=1,
            grid=(KVH, count),
            in_specs=[
                pl.BlockSpec((rows, width), by_head),
                pl.BlockSpec((rows, width), by_head),
                pl.BlockSpec((rows, width), by_head),
                pl.BlockSpec((1, 1, G * rows), lambda h, j, meta_ref: (h, 0, 0)),
                pl.BlockSpec((1, rows), whole),
            ]
            + kv_specs(count, rows)
            + [pl.BlockSpec((rows, HD), whole)] * 2,
            out_specs=[pl.BlockSpec((rows, width), by_head), own, own, far, far],
            scratch_shapes=[
                pltpu.VMEM((G * rows, HD), BF),
                pltpu.VMEM((G * rows, HD), BF),
                pltpu.VMEM((1, G * rows), F32),
                pltpu.VMEM((HD, G * rows), F32),
            ],
        ),
        out_shape=[jax.ShapeDtypeStruct((rows, H * HD), BF)]
        + [jax.ShapeDtypeStruct((chips, rows, KVH * HD), BF)] * 4,
        compiler_params=pltpu.CompilerParams(vmem_limit_bytes=VMEM_LIMIT),
        cost_estimate=pl.CostEstimate(
            flops=400 * rows * rows * count * H * HD,
            bytes_accessed=count * rows * 1024,
            transcendentals=rows * rows * count * H,
        ),
    )(meta, qkv, dout, att, lse, starts, line, line, other, other, cosine, sine)


def assemble_kernel(packs, depth, at_ref, *refs):
    *sources, out_ref, sems = refs
    chips = sources[0].shape[0]
    chip, core, pack = at_ref[0], at_ref[1], at_ref[2]
    copies = []
    for n, source in enumerate(sources):
        k, other = n // 2, n % 2
        for s in range(chips):
            place = lax.rem(chip - s + chips, chips) * 2 + (core ^ other)
            start = pl.multiple_of((place * packs + (pack ^ k)) * depth, depth)
            copies.append(
                pltpu.make_async_copy(
                    source.at[s, pl.ds(0, depth)],
                    out_ref.at[pl.ds(start, depth)],
                    sems.at[len(copies)],
                )
            )
    for copy in copies:
        copy.start()
    for copy in copies:
        copy.wait()


def assemble(place, lines, depth):
    chips, _, cols = lines[0].shape
    count = len(lines) * chips
    if depth % 16:
        out = jnp.zeros((count, depth, cols), lines[0].dtype)
        for n, line in enumerate(lines):
            for s in range(chips):
                where = (place.chip_at(-s) * 2 + (place.core ^ (n % 2))) * place.packs
                out = put(out, line[s, :depth], where + (place.pack ^ (n // 2)))
        return out.reshape(count * depth, cols)
    at = jnp.stack([place.chip, place.core, place.pack]).astype(jnp.int32)
    return pl.pallas_call(
        functools.partial(assemble_kernel, place.packs, depth),
        grid_spec=pltpu.PrefetchScalarGridSpec(
            num_scalar_prefetch=1,
            grid=(1,),
            in_specs=[pl.BlockSpec(memory_space=pl.ANY)] * len(lines),
            out_specs=pl.BlockSpec((count * depth, cols), lambda i, at_ref: (0, 0)),
            scratch_shapes=[pltpu.SemaphoreType.DMA((count,))],
        ),
        out_shape=jax.ShapeDtypeStruct((count * depth, cols), lines[0].dtype),
        compiler_params=pltpu.CompilerParams(vmem_limit_bytes=VMEM_LIMIT),
        cost_estimate=pl.CostEstimate(
            flops=0, bytes_accessed=4 * count * depth * cols, transcendentals=0
        ),
    )(at, *lines)


def feed_kernel(
    h0_ref, h1_ref, t0_ref, t1_ref, gate_ref, up_ref, down_ref, *refs
):
    act0_ref, dgate0_ref, dup0_ref, act1_ref, dgate1_ref, dup1_ref, own_ref, other_ref, h, t = refs[-10:]
    rows = h0_ref.shape[1]
    h[:rows], h[rows:] = h0_ref[0], h1_ref[0]
    t[:rows], t[rows:] = t0_ref[0], t1_ref[0]
    gate = matmul(h[...], gate_ref[...])
    up = matmul(h[...], up_ref[...])
    dact = matmul_nt(t[...], down_ref[...])
    sig = 1.0 / (1.0 + jnp.exp(-gate))
    silu = gate * sig
    act = (silu * up).astype(BF)
    dgate = (dact * up * (sig * (1.0 + gate * (1.0 - sig)))).astype(BF)
    dup = (dact * silu).astype(BF)
    act0_ref[0], act1_ref[0] = act[:rows], act[rows:]
    dgate0_ref[0], dgate1_ref[0] = dgate[:rows], dgate[rows:]
    dup0_ref[0], dup1_ref[0] = dup[:rows], dup[rows:]
    part = matmul_nt(dgate, gate_ref[...]) + matmul_nt(dup, up_ref[...])
    own_ref[0] = part[:rows]
    other_ref[0] = part[rows:].astype(BF)


def feed(hs, ts, gate_w, up_w, down):
    count, rows, width = hs[0].shape
    ff = gate_w.shape[1]
    entry = lambda i: (i, 0, 0)
    whole = lambda i: (0, 0)
    once = pl.Buffered(1)
    tokens = pl.BlockSpec((1, rows, width), entry)
    column = pl.BlockSpec((1, rows, ff), entry)
    return pl.pallas_call(
        feed_kernel,
        grid=(count,),
        in_specs=[tokens] * 4
        + [
            pl.BlockSpec((width, ff), whole, pipeline_mode=once),
            pl.BlockSpec((width, ff), whole, pipeline_mode=once),
            pl.BlockSpec((ff, width), whole, pipeline_mode=once),
        ],
        out_specs=[column] * 6 + [tokens] * 2,
        out_shape=[jax.ShapeDtypeStruct((count, rows, ff), BF)] * 6
        + [
            jax.ShapeDtypeStruct((count, rows, width), F32),
            jax.ShapeDtypeStruct((count, rows, width), BF),
        ],
        scratch_shapes=[pltpu.VMEM((2 * rows, width), BF)] * 2,
        compiler_params=pltpu.CompilerParams(vmem_limit_bytes=VMEM_LIMIT),
        cost_estimate=pl.CostEstimate(
            flops=75 * count * rows * width * ff,
            bytes_accessed=6 * width * ff,
            transcendentals=2 * count * rows * ff,
        ),
    )(*hs, *ts, gate_w, up_w, down)


def grads_kernel(packs, n, *refs):
    *refs, out_ref = refs
    _, near, _, depth, ff = out_ref.shape
    for i in range(2):
        grad = sum(matmul_tn(refs[j][...], refs[n + i * n + j][...]) for j in range(n))
        grad = grad.astype(BF).reshape(near, packs, depth, ff)
        for p in range(packs):
            out_ref[p, :, i] = grad[:, p]


def gate_up_grads(blocks, packs, depth, ff, hs, dgates, dups):
    width = hs[0].shape[1]
    tile = width // 4
    if depth % 16 or tile % (packs * depth):
        grads = [sum(matmul_tn(h, d) for h, d in zip(hs, ds)).astype(BF) for ds in (dgates, dups)]
        return jnp.stack(grads).reshape(2, blocks, packs, depth, ff).transpose(2, 1, 0, 3, 4)
    near = tile // (packs * depth)
    columns = [pl.BlockSpec((h.shape[0], tile), lambda j: (0, j)) for h in hs]
    once = pl.Buffered(1)
    kept = [pl.BlockSpec(d.shape, lambda j: (0, 0), pipeline_mode=once) for d in dgates + dups]
    rows = sum(h.shape[0] for h in hs)
    return pl.pallas_call(
        functools.partial(grads_kernel, packs, len(hs)),
        grid=(4,),
        in_specs=columns + kept,
        out_specs=pl.BlockSpec((packs, near, 2, depth, ff), lambda j: (0, j, 0, 0, 0)),
        out_shape=jax.ShapeDtypeStruct((packs, blocks, 2, depth, ff), BF),
        compiler_params=pltpu.CompilerParams(vmem_limit_bytes=VMEM_LIMIT),
        cost_estimate=pl.CostEstimate(
            flops=7 * rows * width * ff, bytes_accessed=6 * rows * ff, transcendentals=0
        ),
    )(*hs, *dgates, *dups)


def down_grads_kernel(n, *refs):
    *refs, out_ref = refs
    out_ref[...] = sum(matmul_tn(refs[j][...], refs[n + j][...]) for j in range(n)).astype(BF)


def down_grads(acts, tops):
    ff, width = acts[0].shape[1], tops[0].shape[1]
    tile = width // 4
    rows = sum(act.shape[0] for act in acts)
    once = pl.Buffered(1)
    return pl.pallas_call(
        functools.partial(down_grads_kernel, len(acts)),
        grid=(4,),
        in_specs=[pl.BlockSpec(act.shape, lambda j: (0, 0), pipeline_mode=once) for act in acts]
        + [pl.BlockSpec((top.shape[0], tile), lambda j: (0, j)) for top in tops],
        out_specs=pl.BlockSpec((ff, tile), lambda j: (0, j)),
        out_shape=jax.ShapeDtypeStruct((ff, width), BF),
        compiler_params=pltpu.CompilerParams(vmem_limit_bytes=VMEM_LIMIT),
        cost_estimate=pl.CostEstimate(
            flops=2 * rows * width * ff, bytes_accessed=4 * rows * width, transcendentals=0
        ),
    )(*acts, *tops)


def on_device(
    tokens, lengths, out_grad, w_qkv, b_qkv, w_out, gain_attn, w_gate, w_up, w_down, gain_mlp
):
    rows, width = tokens.shape[1:]
    place = Place()
    blocks, packs, chips = place.blocks, place.packs, place.chips
    blk, chip, core = place.blk, place.chip, place.core
    depth = w_qkv.shape[0]
    qkv_cols = w_qkv.shape[1]
    ff = w_gate.shape[1] // blocks
    q_cols = H * HD

    token_index = blk * rows + jnp.arange(rows, dtype=jnp.int32)
    ends = jnp.cumsum(lengths[0])
    doc_starts = ends - lengths[0]
    inside = (token_index[:, None] >= doc_starts[None, :]) & (token_index[:, None] < ends[None, :])
    begin = jnp.sum(jnp.where(inside, doc_starts[None, :], 0), axis=1)
    half = HD // 2
    freq = 10000.0 ** (-2.0 * jnp.arange(half, dtype=F32) / HD)
    angle = (token_index - begin).astype(F32)[:, None] * freq[None, :]
    cosine, sine = jnp.cos(angle), jnp.sin(angle)
    cosine = jnp.concatenate([cosine, cosine], axis=1)
    sine = jnp.concatenate([-sine, sine], axis=1)
    starts = begin[None, :].astype(jnp.int32)

    bias_n, gain_n = b_qkv.shape[0], gain_attn.shape[0]
    shard = blk * packs + place.pack

    def placed(vector):
        row = jnp.zeros((qkv_cols,), BF)
        return lax.dynamic_update_slice(row, vector.astype(BF), (shard * vector.shape[0],))

    spare = jnp.stack([placed(b_qkv), placed(gain_attn), placed(gain_mlp)])
    spare = jnp.pad(spare, ((0, 5), (0, 0)))
    line = gather_line(jnp.concatenate([w_qkv.astype(BF), spare]))
    grad_top = out_grad[0]
    gate_up = jnp.stack([w_gate, w_up]).astype(BF).reshape(2, depth, chips, 2, ff)
    gate_up = after(gate_up.transpose(2, 3, 0, 1, 4), line)
    lines = [line] + [pack_swap(line, k) for k in range(1, packs)]
    lines = [piece for line in lines for piece in (line, core_swap(after(line, lines[1])))]
    gate_up = exchange_cores(place, after(exchange_chips(place, gate_up), lines))
    gate_up = gate_up.reshape(blocks, 2, depth, ff)
    vectors = jnp.sum(sum(piece[:, depth:].astype(F32) for piece in lines), axis=0)
    bias = vectors[:1]
    attn_gain, mlp_gain = vectors[1, :width], vectors[2, :width]
    out_line = gather_line(after(w_out.astype(BF), gate_up))
    qkv_full = assemble(place, lines, depth)

    down = lax.all_gather(after(w_down, lines[2]).astype(BF), "pack", axis=0, tiled=True)
    out_lines = [out_line] + [pack_swap(out_line, k) for k in range(1, packs)]

    def whole(part):
        part = lax.all_gather(part.reshape(blocks * depth, ff), "pack", axis=0, tiled=True)
        part = part.reshape(packs, blocks, depth, ff).transpose(1, 0, 2, 3)
        return part.reshape(width, ff)

    gate_w, up_w = whole(gate_up[:, 0]), whole(gate_up[:, 1])

    stream = tokens[0].astype(F32)
    normed = rms_norm(stream, attn_gain).astype(BF)
    qkv = qkv_project(normed, qkv_full, bias, cosine, sine)
    own = qkv[:, q_cols:]
    kv_line = jnp.stack([own] + [chip_shift(own, s, cyclic=False) for s in range(1, chips)])
    top = after(out_grad[0], gate_up)
    t = {0: grad_top, 1: chip_shift(top, 1)}
    if chips > 2:
        t[chips - 1] = chip_shift(top, -1)
    kv_other = core_swap(after(kv_line, out_lines))
    back = jnp.arange(chips, dtype=jnp.int32)
    source = jnp.concatenate([(chip - back) * 2 + core, (chip - back) * 2 + 1 - core])
    valid = ((source >= 0) & (source <= blk)).astype(jnp.int32)
    clear = ((source < blk) & (source * rows >= jnp.max(begin))).astype(jnp.int32)
    meta = jnp.concatenate([(blk * rows)[None], valid * (1 + clear), source * rows])
    meta = meta.astype(jnp.int32)
    att, att_low, lse = attention_forward(meta, qkv, starts, kv_line, kv_other)
    out_lines = after(out_lines, att_low)
    out_lines = [piece for line in out_lines for piece in (line, core_swap(line))]
    out_full = assemble(place, out_lines, depth)
    for s in range(2, chips - 1):
        t[s] = chip_shift(t[s - 1], 1)
    att_low = after(att_low, t)
    middle = stream + matmul(att_low, out_full)

    hidden = rms_norm(middle, mlp_gain).astype(BF)

    normed_all = lax.all_gather(after(normed, up_w, down), "pack", axis=0, tiled=True)
    att_all = lax.all_gather(after(att_low, up_w, down), "pack", axis=0, tiled=True)

    def both(blocks):
        line = jnp.stack(blocks)
        return line, core_swap(line)

    def pass_back(parts):
        parts = dict(parts)
        for s in reversed(range(2, chips - 1)):
            parts[s - 1] = parts[s - 1] + chip_shift(parts[s].astype(BF), -1).astype(F32)
        return parts

    def give_back(parts):
        total = parts[0] + chip_shift(parts[1].astype(BF), -1).astype(F32)
        if chips > 2:
            total = total + chip_shift(parts[chips - 1].astype(BF), 1).astype(F32)
        return total

    h = {0: hidden, 1: chip_shift(hidden, 1)}
    if chips > 2:
        h[chips - 1] = chip_shift(hidden, -1)
    for s in range(2, chips - 1):
        h[s] = chip_shift(h[s - 1], 1)
    h[0], h[chips - 1] = after((h[0], h[chips - 1]), h[chips - 1])
    h[1] = after(h[1], h[chips - 1])
    first, second = (list(range(chips - 2, 0, -1)), [chips - 1, 0]) if chips > 2 else ([1, 0], [])
    hs, ts, fed, partials = [], [], [], {}
    for part in (first, second):
        if not part:
            continue
        h_pair, t_pair = both([h[s] for s in part]), both([t[s] for s in part])
        if partials:
            h_pair = after(h_pair, mine)
        *kept, mine, other = feed(h_pair, t_pair, gate_w, up_w, down)
        mine = mine + core_swap(other).astype(F32)
        partials.update({s: mine[i] for i, s in enumerate(part)})
        flat = lambda arrays: [one.reshape(len(part) * rows, -1) for one in arrays]
        hs, ts = hs + flat(h_pair), ts + flat(t_pair)
        fed.append(flat(kept))
    acts, dgates, dups = ([one for kept in fed for one in kept[i::3]] for i in range(3))
    partials = pass_back(partials)
    hs = after(hs, partials)
    grad_hidden = give_back(partials)

    grad_gu = gate_up_grads(blocks, packs, depth, ff, hs, dgates, dups)
    out_parts, outs = [matmul(act, down) for act in after(acts, grad_gu)], {}
    for i, part in enumerate((first, second)):
        if part:
            other = core_swap(out_parts[2 * i + 1].astype(BF))
            mine = (out_parts[2 * i] + other.astype(F32)).reshape(len(part), rows, width)
            outs.update({s: mine[n] for n, s in enumerate(part)})
    grad_hidden = after(grad_hidden, grad_gu)

    grad_gu = after(grad_gu, normed_all, att_all).reshape(packs * blocks * 2 * depth, ff)
    grad_gu = lax.psum_scatter(grad_gu, "pack", scatter_dimension=0, tiled=True)

    _, second_pull = jax.vjp(rms_norm, middle, mlp_gain)
    grad_mid, grad_mlp_gain = second_pull(grad_hidden)
    grad_middle = grad_top.astype(F32) + grad_mid

    middle_low = grad_middle.astype(BF)

    dout = matmul_nt(middle_low, out_full).astype(BF).reshape(rows, q_cols)
    dout, outs = after((dout, outs), dout, outs)
    outs = pass_back(outs)
    if chips > 2:
        outs[chips - 1] = chip_shift(outs[chips - 1].astype(BF), 1)
    dq, dk0, dv0, dk1, dv1 = attention_backward(
        meta, qkv, dout, att, lse, starts, kv_line, kv_other, cosine, sine
    )
    dk1, dv1, outs = after((dk1, dv1, outs), outs)
    result = middle + outs[0] + chip_shift(outs[1].astype(BF), -1).astype(F32)
    if chips > 2:
        result = result + outs[chips - 1].astype(F32)
    result = result.astype(BF)
    other = core_swap(jnp.concatenate([dk1, dv1], axis=2))
    mine = jnp.concatenate([dk0, dv0], axis=2).astype(F32) + other.astype(F32)
    acts, ts = after((acts, ts), mine)
    grad_down = down_grads(acts, ts)
    sent = [by_columns(middle_low, packs), by_columns(after(dq, grad_down), packs)]
    got = exchange_packs(place, jnp.concatenate(sent, axis=2))
    got = jnp.concatenate(in_pack_order(place, got))
    part = width // packs
    parts = [matmul_tn(att_all, got[:, :part]), matmul_tn(normed_all, got[:, part:])]
    parts = jnp.concatenate(parts, axis=1).astype(BF)
    pair = mine[0]
    for s in range(1, chips):
        pair = pair + chip_shift(mine[s].astype(BF), -s, cyclic=False).astype(F32)
    turned = []
    for j in range(KVH):
        one = pair[:, j * HD : (j + 1) * HD]
        swapped = jnp.concatenate([one[:, half:], one[:, :half]], axis=1)
        turned.append(one * cosine - swapped * sine)
    dkv = jnp.concatenate(turned + [pair[:, KVH * HD :]], axis=1).astype(BF)
    gu_here = exchange_chips(place, grad_gu.reshape(chips, 2, 2, depth, ff))
    parts = reduce_line(place, parts.reshape(chips, 2, packs * depth, -1), gu_here).astype(BF)
    gu_here = exchange_cores(place, gu_here)
    parts = after(parts, dkv, result)
    got = exchange_packs(place, parts.reshape(packs, depth, -1))
    got = in_pack_order(place, got)
    grad_out_w = jnp.concatenate([piece[:, :part] for piece in got], axis=1).astype(F32)
    grad_q = jnp.concatenate([piece[:, part:] for piece in got], axis=1).astype(F32)
    grad_down = lax.psum_scatter(grad_down, "pack", scatter_dimension=0, tiled=True).astype(F32)
    grad_gu = gu_here.reshape(blocks, 2, depth, ff).transpose(1, 2, 0, 3).reshape(2, depth, -1)
    grad_gate_w, grad_up_w = grad_gu[0].astype(F32), grad_gu[1].astype(F32)
    dproj = jnp.concatenate([dq, dkv], axis=1)

    grad_normed = matmul_nt(dproj, qkv_full)
    _, first_pull = jax.vjp(rms_norm, stream, attn_gain)
    grad_input, grad_attn_gain = first_pull(grad_normed)
    input_grad = (grad_middle + grad_input).astype(BF)
    grad_bias = jnp.sum(dproj.astype(F32), axis=0)
    vector_grads = jnp.concatenate(
        [
            grad_bias.reshape(-1, bias_n),
            grad_attn_gain.reshape(-1, gain_n),
            grad_mlp_gain.reshape(-1, gain_n),
        ],
        axis=1,
    ).astype(BF)
    part = (qkv_cols - q_cols) // packs
    lines = -(-vector_grads.shape[1] // part)
    lines += -(blocks * lines) % 16 // blocks
    vector_grads = jnp.pad(vector_grads, ((0, 0), (0, lines * part - vector_grads.shape[1])))
    vector_grads = vector_grads.reshape(blocks, packs, lines, part).transpose(1, 0, 2, 3)
    vector_grads = vector_grads.reshape(packs, blocks * lines, part)
    got = exchange_packs(place, jnp.concatenate([by_columns(dkv, packs), vector_grads], axis=1))
    kv_all = jnp.concatenate(in_pack_order(place, [piece[:rows] for piece in got]))
    grad_kv = matmul_tn(normed_all, kv_all).astype(BF)
    vector_sum = sum(piece[rows:].astype(F32) for piece in got).astype(BF)
    grad_kv = jnp.concatenate(
        [grad_kv.reshape(blocks, packs * depth, part), vector_sum.reshape(blocks, lines, part)],
        axis=1,
    )
    grad_kv = reduce_line(place, grad_kv.reshape(chips, 2, -1, part))
    tail = grad_kv[packs * depth :].reshape(-1)
    grad_kv = to_shard(place, grad_kv[: packs * depth].astype(BF), depth)
    return (
        result[None],
        input_grad[None],
        jnp.concatenate([grad_q, grad_kv], axis=1),
        tail[:bias_n],
        grad_out_w,
        tail[bias_n : bias_n + gain_n],
        grad_gate_w,
        grad_up_w,
        grad_down,
        tail[bias_n + gain_n : bias_n + 2 * gain_n],
    )


def solution(mesh):
    tokens, rows, vector = P("pack", "blk", None), P(BOTH, None), P(BOTH)
    in_specs = (
        tokens, P("pack", None), tokens, rows, vector, rows, vector, rows, rows, rows, vector
    )
    out_specs = (tokens, tokens, rows, vector, rows, vector, rows, rows, rows, vector)
    return jax.shard_map(
        on_device, mesh=mesh, in_specs=in_specs, out_specs=out_specs, check_vma=False
    )
```

```python
import functools

import jax
import jax.numpy as jnp
from jax import lax
from jax.experimental import pallas as pl
from jax.experimental.pallas import tpu as pltpu
from jax.sharding import PartitionSpec as P

H = 12
KVH = 2
HD = 128
G = H // KVH
NEG = -1e30
BF = jnp.bfloat16
F32 = jnp.float32
VMEM_LIMIT = 56 * 1024 * 1024
BOTH = ("blk", "pack")


def chip_shift(block, by, cyclic=True):
    n = lax.axis_size("blk")
    route = [(i, (i + 2 * by) % n) for i in range(n) if cyclic or 0 <= i + 2 * by < n]
    return lax.ppermute(block, "blk", route)


def core_swap(block):
    n = lax.axis_size("blk")
    return lax.ppermute(block, "blk", [(i, i ^ 1) for i in range(n)])


def pack_swap(block, k):
    n = lax.axis_size("pack")
    return lax.ppermute(block, "pack", [(i, i ^ k) for i in range(n)])


def put(buffer, piece, *index):
    piece = piece.reshape((1,) * len(index) + piece.shape)
    zeros = (0,) * (buffer.ndim - len(index))
    return lax.dynamic_update_slice(buffer, piece, tuple(index) + zeros)


def take(array, axis, index):
    return lax.dynamic_index_in_dim(array, index, axis, keepdims=False)


class Place:
    def __init__(self):
        self.blocks, self.packs = lax.axis_size("blk"), lax.axis_size("pack")
        self.chips = self.blocks // 2
        self.blk, self.pack = lax.axis_index("blk"), lax.axis_index("pack")
        self.chip, self.core = self.blk // 2, self.blk % 2

    def chip_at(self, by):
        return lax.rem(self.chip + by + self.chips, self.chips)


def in_core_order(place, mine, other):
    first = jnp.where(place.core == 0, mine, other)
    second = jnp.where(place.core == 0, other, mine)
    return jnp.stack([first, second], axis=1)


def after(value, *before):
    return lax.optimization_barrier((value, before))[0]


def gather_line(block):
    chips = lax.axis_size("blk") // 2
    return jnp.stack([block] + [chip_shift(block, s) for s in range(1, chips)])


def exchange_packs(place, parts):
    got = [take(parts, 0, place.pack)]
    for k in range(1, place.packs):
        got.append(pack_swap(take(parts, 0, place.pack ^ k), k))
    return got


def reduce_line(place, parts, before=()):
    other = core_swap(take(parts, 1, 1 - place.core))
    mine = after(take(parts, 1, place.core).astype(F32) + other.astype(F32), before)
    line = mine.astype(BF)
    total = take(mine, 0, place.chip)
    for s in range(1, place.chips):
        total = total + chip_shift(take(line, 0, place.chip_at(s)), s).astype(F32)
    return total


def by_columns(matrix, packs):
    return jnp.stack(jnp.split(matrix, packs, axis=1))


def in_pack_order(place, pieces):
    ordered = []
    for q in range(place.packs):
        chosen = pieces[q]
        for p in range(1, place.packs):
            chosen = jnp.where(place.pack == p, pieces[q ^ p], chosen)
        ordered.append(chosen)
    return ordered


def to_shard(place, grad, depth):
    pieces = exchange_packs(place, grad.reshape(place.packs, depth, -1))
    return jnp.concatenate(in_pack_order(place, pieces), axis=1).astype(F32)


def exchange_chips(place, parts):
    got = jnp.zeros(parts.shape, parts.dtype)
    got = put(got, take(parts, 0, place.chip), place.chip)
    for s in range(1, place.chips):
        got = put(got, chip_shift(take(parts, 0, place.chip_at(s)), s), place.chip_at(-s))
    return got


def exchange_cores(place, got):
    other = core_swap(take(got, 1, 1 - place.core))
    return in_core_order(place, take(got, 1, place.core), other)


def matmul(left, right):
    return jnp.dot(left, right, preferred_element_type=F32)


def matmul_tn(left, right):
    return lax.dot_general(left, right, (((0,), (0,)), ((), ())), preferred_element_type=F32)


def matmul_nt(left, right):
    return lax.dot_general(left, right, (((1,), (1,)), ((), ())), preferred_element_type=F32)


def rms_norm(values, gain):
    return values * lax.rsqrt(jnp.mean(values * values, axis=-1, keepdims=True) + 1e-06) * gain


def turn(x, cosine, sine):
    return x * cosine + pltpu.roll(x, HD // 2, 1) * sine


def qkv_kernel(xn_ref, w_ref, bias_ref, cos_ref, sin_ref, out_ref):
    step = pl.program_id(0)
    proj = matmul(xn_ref[...], w_ref[...]) + bias_ref[...]
    cosine, sine = cos_ref[...], sin_ref[...]

    @pl.when(step < H // 2)
    def _():
        for i in range(2):
            cut = slice(i * HD, (i + 1) * HD)
            out_ref[:, cut] = (turn(proj[:, cut], cosine, sine) * HD**-0.5).astype(BF)

    @pl.when((step >= H // 2) & (step < (H + KVH) // 2))
    def _():
        for i in range(2):
            cut = slice(i * HD, (i + 1) * HD)
            out_ref[:, cut] = turn(proj[:, cut], cosine, sine).astype(BF)

    @pl.when(step >= (H + KVH) // 2)
    def _():
        out_ref[...] = proj.astype(BF)


def qkv_project(xn, w, bias, cosine, sine):
    rows, depth = xn.shape
    cols = w.shape[1]
    return pl.pallas_call(
        qkv_kernel,
        grid=(cols // 256,),
        in_specs=[
            pl.BlockSpec((rows, depth), lambda i: (0, 0)),
            pl.BlockSpec((depth, 256), lambda i: (0, i)),
            pl.BlockSpec((1, 256), lambda i: (0, i)),
            pl.BlockSpec((rows, HD), lambda i: (0, 0)),
            pl.BlockSpec((rows, HD), lambda i: (0, 0)),
        ],
        out_specs=pl.BlockSpec((rows, 256), lambda i: (0, i)),
        out_shape=jax.ShapeDtypeStruct((rows, cols), BF),
        compiler_params=pltpu.CompilerParams(vmem_limit_bytes=VMEM_LIMIT),
        cost_estimate=pl.CostEstimate(
            flops=2 * rows * depth * cols, bytes_accessed=2 * depth * cols, transcendentals=0
        ),
    )(xn, w, bias, cosine, sine)


def allowed_mask(meta_ref, starts_ref, slot, count):
    rows, lanes = starts_ref.shape[1], G * starts_ref.shape[1]
    starts = jnp.concatenate([starts_ref[...]] * G, axis=1)
    key_index = meta_ref[1 + count + slot] + lax.broadcasted_iota(jnp.int32, (rows, lanes), 0)
    query = lax.rem(lax.broadcasted_iota(jnp.int32, (1, lanes), 1), rows)
    return (key_index >= starts) & (key_index <= meta_ref[0] + query)


def stack_heads(target, source_ref):
    rows = source_ref.shape[0]
    for g in range(G):
        target[g * rows : (g + 1) * rows, :] = source_ref[:, g * HD : (g + 1) * HD]


def when_needed(meta_ref, count, work, pieces):
    slot = pl.program_id(1)
    state = meta_ref[1 + slot]
    for core, (k_ref, v_ref) in enumerate(pieces):
        here = slot < count // 2 if core == 0 else slot >= count // 2
        for masked in (True, False):

            @pl.when(here & (state == (1 if masked else 2)))
            def _(k_ref=k_ref, v_ref=v_ref, masked=masked):
                work(k_ref[0], v_ref[0], masked)


def forward_kernel(
    count, meta_ref, q_ref, starts_ref, k0_ref, v0_ref, k1_ref, v1_ref,
    att_ref, low_ref, lse_ref, q, m, total, acc,
):
    slot = pl.program_id(1)
    rows = q_ref.shape[0]

    @pl.when(slot == 0)
    def _():
        stack_heads(q, q_ref)
        m[...] = jnp.full(m.shape, NEG, F32)
        total[...] = jnp.zeros(total.shape, F32)
        acc[...] = jnp.zeros(acc.shape, F32)

    def work(keys, values, masked):
        scores = matmul_nt(keys, q[...])
        if masked:
            scores = jnp.where(allowed_mask(meta_ref, starts_ref, slot, count), scores, NEG)
        before = m[...]
        now = jnp.maximum(before, jnp.max(scores, axis=0, keepdims=True))
        weights = jnp.exp(scores - now)
        fade = jnp.exp(before - now)
        m[...] = now
        total[...] = total[...] * fade + jnp.sum(weights, axis=0, keepdims=True)
        acc[...] = acc[...] * fade + matmul_tn(values, weights.astype(BF))

    when_needed(meta_ref, count, work, ((k0_ref, v0_ref), (k1_ref, v1_ref)))

    @pl.when(slot == count - 1)
    def _():
        out = acc[...] / total[...]
        for g in range(G):
            head = out[:, g * rows : (g + 1) * rows].T
            att_ref[:, g * HD : (g + 1) * HD] = head
            low_ref[:, g * HD : (g + 1) * HD] = head.astype(BF)
        lse_ref[0] = m[...] + jnp.log(total[...])


def kv_specs(count, rows):
    half = count // 2
    specs = []
    for core in range(2):
        for first in (0, KVH):

            def where(h, j, meta_ref, core=core, first=first):
                here = (j < half) if core == 0 else (j >= half)
                index = jnp.where(here & (meta_ref[1 + j] > 0), j - core * half, 0)
                return (index, 0, first + h)

            specs.append(pl.BlockSpec((1, rows, HD), where))
    return specs


def attention_forward(meta, qkv, starts, line, other):
    count, rows = 2 * line.shape[0], line.shape[1]
    width = G * HD
    by_head = lambda h, j, meta_ref: (0, h)
    return pl.pallas_call(
        functools.partial(forward_kernel, count),
        grid_spec=pltpu.PrefetchScalarGridSpec(
            num_scalar_prefetch=1,
            grid=(KVH, count),
            in_specs=[
                pl.BlockSpec((rows, width), by_head),
                pl.BlockSpec((1, rows), lambda h, j, meta_ref: (0, 0)),
            ]
            + kv_specs(count, rows),
            out_specs=[
                pl.BlockSpec((rows, width), by_head),
                pl.BlockSpec((rows, width), by_head),
                pl.BlockSpec((1, 1, G * rows), lambda h, j, meta_ref: (h, 0, 0)),
            ],
            scratch_shapes=[
                pltpu.VMEM((G * rows, HD), BF),
                pltpu.VMEM((1, G * rows), F32),
                pltpu.VMEM((1, G * rows), F32),
                pltpu.VMEM((HD, G * rows), F32),
            ],
        ),
        out_shape=[
            jax.ShapeDtypeStruct((rows, H * HD), F32),
            jax.ShapeDtypeStruct((rows, H * HD), BF),
            jax.ShapeDtypeStruct((KVH, 1, G * rows), F32),
        ],
        compiler_params=pltpu.CompilerParams(vmem_limit_bytes=VMEM_LIMIT),
        cost_estimate=pl.CostEstimate(
            flops=16 * rows * rows * count * H * HD,
            bytes_accessed=count * rows * 1024,
            transcendentals=rows * rows * count * H,
        ),
    )(meta, qkv, starts, line, line, other, other)


def backward_kernel(
    count, meta_ref, q_ref, dout_ref, att_ref, lse_ref, starts_ref, k0_ref, v0_ref, k1_ref, v1_ref,
    cos_ref, sin_ref, dq_ref, dk0_ref, dv0_ref, dk1_ref, dv1_ref, q, dout, delta, dq_sum,
):
    slot = pl.program_id(1)
    rows = q_ref.shape[0]
    half = count // 2

    @pl.when(slot == 0)
    def _():
        stack_heads(q, q_ref)
        stack_heads(dout, dout_ref)
        dq_sum[...] = jnp.zeros(dq_sum.shape, F32)
        for g in range(G):
            cut = slice(g * HD, (g + 1) * HD)
            product = dout_ref[:, cut].astype(F32) * att_ref[:, cut]
            delta[:, g * rows : (g + 1) * rows] = jnp.sum(product.T, axis=0, keepdims=True)

    def work(keys, values, masked):
        weights = jnp.exp(matmul_nt(keys, q[...]) - lse_ref[0])
        if masked:
            weights = jnp.where(allowed_mask(meta_ref, starts_ref, slot, count), weights, 0.0)
        dv = matmul(weights.astype(BF), dout[...]).astype(BF)
        dscores = (weights * (matmul_nt(values, dout[...]) - delta[...])).astype(BF)
        dk = matmul(dscores, q[...]).astype(BF)
        dq_sum[...] = dq_sum[...] + matmul_tn(keys, dscores)

        @pl.when(slot < half)
        def _():
            dk0_ref[0], dv0_ref[0] = dk, dv

        @pl.when(slot >= half)
        def _():
            dk1_ref[0], dv1_ref[0] = dk, dv

    @pl.when((meta_ref[1 + slot] == 0) & (slot < half))
    def _():
        dk0_ref[...] = jnp.zeros(dk0_ref.shape, BF)
        dv0_ref[...] = jnp.zeros(dv0_ref.shape, BF)

    @pl.when((meta_ref[1 + slot] == 0) & (slot >= half))
    def _():
        dk1_ref[...] = jnp.zeros(dk1_ref.shape, BF)
        dv1_ref[...] = jnp.zeros(dv1_ref.shape, BF)

    when_needed(meta_ref, count, work, ((k0_ref, v0_ref), (k1_ref, v1_ref)))

    @pl.when(slot == count - 1)
    def _():
        for g in range(G):
            back = dq_sum[:, g * rows : (g + 1) * rows].T * HD**-0.5
            dq_ref[:, g * HD : (g + 1) * HD] = turn(back, cos_ref[...], -sin_ref[...]).astype(BF)


def attention_backward(meta, qkv, dout, att, lse, starts, line, other, cosine, sine):
    chips, rows = line.shape[:2]
    count = 2 * chips
    width = G * HD
    whole = lambda h, j, meta_ref: (0, 0)
    by_head = lambda h, j, meta_ref: (0, h)
    own = pl.BlockSpec((1, rows, HD), lambda h, j, meta_ref: (jnp.minimum(j, chips - 1), 0, h))
    far = pl.BlockSpec((1, rows, HD), lambda h, j, meta_ref: (jnp.maximum(j - chips, 0), 0, h))
    return pl.pallas_call(
        functools.partial(backward_kernel, count),
        grid_spec=pltpu.PrefetchScalarGridSpec(
            num_scalar_prefetch=1,
            grid=(KVH, count),
            in_specs=[
                pl.BlockSpec((rows, width), by_head),
                pl.BlockSpec((rows, width), by_head),
                pl.BlockSpec((rows, width), by_head),
                pl.BlockSpec((1, 1, G * rows), lambda h, j, meta_ref: (h, 0, 0)),
                pl.BlockSpec((1, rows), whole),
            ]
            + kv_specs(count, rows)
            + [pl.BlockSpec((rows, HD), whole)] * 2,
            out_specs=[pl.BlockSpec((rows, width), by_head), own, own, far, far],
            scratch_shapes=[
                pltpu.VMEM((G * rows, HD), BF),
                pltpu.VMEM((G * rows, HD), BF),
                pltpu.VMEM((1, G * rows), F32),
                pltpu.VMEM((HD, G * rows), F32),
            ],
        ),
        out_shape=[jax.ShapeDtypeStruct((rows, H * HD), BF)]
        + [jax.ShapeDtypeStruct((chips, rows, KVH * HD), BF)] * 4,
        compiler_params=pltpu.CompilerParams(vmem_limit_bytes=VMEM_LIMIT),
        cost_estimate=pl.CostEstimate(
            flops=400 * rows * rows * count * H * HD,
            bytes_accessed=count * rows * 1024,
            transcendentals=rows * rows * count * H,
        ),
    )(meta, qkv, dout, att, lse, starts, line, line, other, other, cosine, sine)


def assemble_kernel(packs, depth, at_ref, *refs):
    *sources, out_ref, sems = refs
    chips = sources[0].shape[0]
    chip, core, pack = at_ref[0], at_ref[1], at_ref[2]
    copies = []
    for n, source in enumerate(sources):
        k, other = n // 2, n % 2
        for s in range(chips):
            place = lax.rem(chip - s + chips, chips) * 2 + (core ^ other)
            start = pl.multiple_of((place * packs + (pack ^ k)) * depth, depth)
            copies.append(
                pltpu.make_async_copy(
                    source.at[s, pl.ds(0, depth)],
                    out_ref.at[pl.ds(start, depth)],
                    sems.at[len(copies)],
                )
            )
    for copy in copies:
        copy.start()
    for copy in copies:
        copy.wait()


def assemble(place, lines, depth):
    chips, _, cols = lines[0].shape
    count = len(lines) * chips
    if depth % 16:
        out = jnp.zeros((count, depth, cols), lines[0].dtype)
        for n, line in enumerate(lines):
            for s in range(chips):
                where = (place.chip_at(-s) * 2 + (place.core ^ (n % 2))) * place.packs
                out = put(out, line[s, :depth], where + (place.pack ^ (n // 2)))
        return out.reshape(count * depth, cols)
    at = jnp.stack([place.chip, place.core, place.pack]).astype(jnp.int32)
    return pl.pallas_call(
        functools.partial(assemble_kernel, place.packs, depth),
        grid_spec=pltpu.PrefetchScalarGridSpec(
            num_scalar_prefetch=1,
            grid=(1,),
            in_specs=[pl.BlockSpec(memory_space=pl.ANY)] * len(lines),
            out_specs=pl.BlockSpec((count * depth, cols), lambda i, at_ref: (0, 0)),
            scratch_shapes=[pltpu.SemaphoreType.DMA((count,))],
        ),
        out_shape=jax.ShapeDtypeStruct((count * depth, cols), lines[0].dtype),
        compiler_params=pltpu.CompilerParams(vmem_limit_bytes=VMEM_LIMIT),
        cost_estimate=pl.CostEstimate(
            flops=0, bytes_accessed=4 * count * depth * cols, transcendentals=0
        ),
    )(at, *lines)


def feed_kernel(
    h0_ref, h1_ref, t0_ref, t1_ref, gate_ref, up_ref, down_ref, *refs
):
    act0_ref, dgate0_ref, dup0_ref, act1_ref, dgate1_ref, dup1_ref, own_ref, other_ref, h, t = refs[-10:]
    rows = h0_ref.shape[1]
    h[:rows], h[rows:] = h0_ref[0], h1_ref[0]
    t[:rows], t[rows:] = t0_ref[0], t1_ref[0]
    gate = matmul(h[...], gate_ref[...])
    up = matmul(h[...], up_ref[...])
    dact = matmul_nt(t[...], down_ref[...])
    sig = 1.0 / (1.0 + jnp.exp(-gate))
    silu = gate * sig
    act = (silu * up).astype(BF)
    dgate = (dact * up * (sig * (1.0 + gate * (1.0 - sig)))).astype(BF)
    dup = (dact * silu).astype(BF)
    act0_ref[0], act1_ref[0] = act[:rows], act[rows:]
    dgate0_ref[0], dgate1_ref[0] = dgate[:rows], dgate[rows:]
    dup0_ref[0], dup1_ref[0] = dup[:rows], dup[rows:]
    part = matmul_nt(dgate, gate_ref[...]) + matmul_nt(dup, up_ref[...])
    own_ref[0] = part[:rows]
    other_ref[0] = part[rows:].astype(BF)


def feed(hs, ts, gate_w, up_w, down):
    count, rows, width = hs[0].shape
    ff = gate_w.shape[1]
    entry = lambda i: (i, 0, 0)
    whole = lambda i: (0, 0)
    once = pl.Buffered(1)
    tokens = pl.BlockSpec((1, rows, width), entry)
    column = pl.BlockSpec((1, rows, ff), entry)
    return pl.pallas_call(
        feed_kernel,
        grid=(count,),
        in_specs=[tokens] * 4
        + [
            pl.BlockSpec((width, ff), whole, pipeline_mode=once),
            pl.BlockSpec((width, ff), whole, pipeline_mode=once),
            pl.BlockSpec((ff, width), whole, pipeline_mode=once),
        ],
        out_specs=[column] * 6 + [tokens] * 2,
        out_shape=[jax.ShapeDtypeStruct((count, rows, ff), BF)] * 6
        + [
            jax.ShapeDtypeStruct((count, rows, width), F32),
            jax.ShapeDtypeStruct((count, rows, width), BF),
        ],
        scratch_shapes=[pltpu.VMEM((2 * rows, width), BF)] * 2,
        compiler_params=pltpu.CompilerParams(vmem_limit_bytes=VMEM_LIMIT),
        cost_estimate=pl.CostEstimate(
            flops=75 * count * rows * width * ff,
            bytes_accessed=6 * width * ff,
            transcendentals=2 * count * rows * ff,
        ),
    )(*hs, *ts, gate_w, up_w, down)


def grads_kernel(packs, n, *refs):
    *refs, out_ref = refs
    _, near, _, depth, ff = out_ref.shape
    for i in range(2):
        grad = sum(matmul_tn(refs[j][...], refs[n + i * n + j][...]) for j in range(n))
        grad = grad.astype(BF).reshape(near, packs, depth, ff)
        for p in range(packs):
            out_ref[p, :, i] = grad[:, p]


def gate_up_grads(blocks, packs, depth, ff, hs, dgates, dups):
    width = hs[0].shape[1]
    tile = width // 4
    if depth % 16 or tile % (packs * depth):
        grads = [sum(matmul_tn(h, d) for h, d in zip(hs, ds)).astype(BF) for ds in (dgates, dups)]
        return jnp.stack(grads).reshape(2, blocks, packs, depth, ff).transpose(2, 1, 0, 3, 4)
    near = tile // (packs * depth)
    columns = [pl.BlockSpec((h.shape[0], tile), lambda j: (0, j)) for h in hs]
    once = pl.Buffered(1)
    kept = [pl.BlockSpec(d.shape, lambda j: (0, 0), pipeline_mode=once) for d in dgates + dups]
    rows = sum(h.shape[0] for h in hs)
    return pl.pallas_call(
        functools.partial(grads_kernel, packs, len(hs)),
        grid=(4,),
        in_specs=columns + kept,
        out_specs=pl.BlockSpec((packs, near, 2, depth, ff), lambda j: (0, j, 0, 0, 0)),
        out_shape=jax.ShapeDtypeStruct((packs, blocks, 2, depth, ff), BF),
        compiler_params=pltpu.CompilerParams(vmem_limit_bytes=VMEM_LIMIT),
        cost_estimate=pl.CostEstimate(
            flops=7 * rows * width * ff, bytes_accessed=6 * rows * ff, transcendentals=0
        ),
    )(*hs, *dgates, *dups)


def down_grads_kernel(n, *refs):
    *refs, out_ref = refs
    out_ref[...] = sum(matmul_tn(refs[j][...], refs[n + j][...]) for j in range(n)).astype(BF)


def down_grads(acts, tops):
    ff, width = acts[0].shape[1], tops[0].shape[1]
    tile = width // 4
    rows = sum(act.shape[0] for act in acts)
    once = pl.Buffered(1)
    return pl.pallas_call(
        functools.partial(down_grads_kernel, len(acts)),
        grid=(4,),
        in_specs=[pl.BlockSpec(act.shape, lambda j: (0, 0), pipeline_mode=once) for act in acts]
        + [pl.BlockSpec((top.shape[0], tile), lambda j: (0, j)) for top in tops],
        out_specs=pl.BlockSpec((ff, tile), lambda j: (0, j)),
        out_shape=jax.ShapeDtypeStruct((ff, width), BF),
        compiler_params=pltpu.CompilerParams(vmem_limit_bytes=VMEM_LIMIT),
        cost_estimate=pl.CostEstimate(
            flops=2 * rows * width * ff, bytes_accessed=4 * rows * width, transcendentals=0
        ),
    )(*acts, *tops)


def on_device(
    tokens, lengths, out_grad, w_qkv, b_qkv, w_out, gain_attn, w_gate, w_up, w_down, gain_mlp
):
    rows, width = tokens.shape[1:]
    place = Place()
    blocks, packs, chips = place.blocks, place.packs, place.chips
    blk, chip, core = place.blk, place.chip, place.core
    depth = w_qkv.shape[0]
    qkv_cols = w_qkv.shape[1]
    ff = w_gate.shape[1] // blocks
    q_cols = H * HD

    token_index = blk * rows + jnp.arange(rows, dtype=jnp.int32)
    ends = jnp.cumsum(lengths[0])
    doc_starts = ends - lengths[0]
    inside = (token_index[:, None] >= doc_starts[None, :]) & (token_index[:, None] < ends[None, :])
    begin = jnp.sum(jnp.where(inside, doc_starts[None, :], 0), axis=1)
    half = HD // 2
    freq = 10000.0 ** (-2.0 * jnp.arange(half, dtype=F32) / HD)
    angle = (token_index - begin).astype(F32)[:, None] * freq[None, :]
    cosine, sine = jnp.cos(angle), jnp.sin(angle)
    cosine = jnp.concatenate([cosine, cosine], axis=1)
    sine = jnp.concatenate([-sine, sine], axis=1)
    starts = begin[None, :].astype(jnp.int32)

    bias_n, gain_n = b_qkv.shape[0], gain_attn.shape[0]
    shard = blk * packs + place.pack

    def placed(vector):
        row = jnp.zeros((qkv_cols,), BF)
        return lax.dynamic_update_slice(row, vector.astype(BF), (shard * vector.shape[0],))

    spare = jnp.stack([placed(b_qkv), placed(gain_attn), placed(gain_mlp)])
    spare = jnp.pad(spare, ((0, 5), (0, 0)))
    line = gather_line(jnp.concatenate([w_qkv.astype(BF), spare]))
    grad_top = out_grad[0]
    gate_up = jnp.stack([w_gate, w_up]).astype(BF).reshape(2, depth, chips, 2, ff)
    gate_up = after(gate_up.transpose(2, 3, 0, 1, 4), line)
    lines = [line] + [pack_swap(line, k) for k in range(1, packs)]
    lines = [piece for line in lines for piece in (line, core_swap(after(line, lines[1])))]
    gate_up = exchange_cores(place, after(exchange_chips(place, gate_up), lines))
    gate_up = gate_up.reshape(blocks, 2, depth, ff)
    vectors = jnp.sum(sum(piece[:, depth:].astype(F32) for piece in lines), axis=0)
    bias = vectors[:1]
    attn_gain, mlp_gain = vectors[1, :width], vectors[2, :width]
    out_line = gather_line(after(w_out.astype(BF), gate_up))
    qkv_full = assemble(place, lines, depth)

    down = lax.all_gather(after(w_down, lines[2]).astype(BF), "pack", axis=0, tiled=True)
    out_lines = [out_line] + [pack_swap(out_line, k) for k in range(1, packs)]

    def whole(part):
        part = lax.all_gather(part.reshape(blocks * depth, ff), "pack", axis=0, tiled=True)
        part = part.reshape(packs, blocks, depth, ff).transpose(1, 0, 2, 3)
        return part.reshape(width, ff)

    gate_w, up_w = whole(gate_up[:, 0]), whole(gate_up[:, 1])

    stream = tokens[0].astype(F32)
    normed = rms_norm(stream, attn_gain).astype(BF)
    top = after(out_grad[0], gate_up)
    t = {0: grad_top, 1: chip_shift(top, 1)}
    if chips > 2:
        t[chips - 1] = chip_shift(top, -1)
    qkv = qkv_project(after(normed, t[1]), qkv_full, bias, cosine, sine)
    own = qkv[:, q_cols:]
    kv_line = jnp.stack([own] + [chip_shift(own, s, cyclic=False) for s in range(1, chips)])
    kv_other = core_swap(after(kv_line, out_lines))
    back = jnp.arange(chips, dtype=jnp.int32)
    source = jnp.concatenate([(chip - back) * 2 + core, (chip - back) * 2 + 1 - core])
    valid = ((source >= 0) & (source <= blk)).astype(jnp.int32)
    clear = ((source < blk) & (source * rows >= jnp.max(begin))).astype(jnp.int32)
    meta = jnp.concatenate([(blk * rows)[None], valid * (1 + clear), source * rows])
    meta = meta.astype(jnp.int32)
    att, att_low, lse = attention_forward(meta, qkv, starts, kv_line, kv_other)
    out_lines = after(out_lines, att_low)
    out_lines = [piece for line in out_lines for piece in (line, core_swap(line))]
    out_full = assemble(place, out_lines, depth)
    for s in range(2, chips - 1):
        t[s] = chip_shift(t[s - 1], 1)
    att_low = after(att_low, t)
    middle = stream + matmul(att_low, out_full)

    hidden = rms_norm(middle, mlp_gain).astype(BF)

    normed_all = lax.all_gather(after(normed, up_w, down), "pack", axis=0, tiled=True)
    att_all = lax.all_gather(after(att_low, up_w, down), "pack", axis=0, tiled=True)

    def both(blocks):
        line = jnp.stack(blocks)
        return line, core_swap(line)

    def pass_back(parts):
        parts = dict(parts)
        for s in reversed(range(2, chips - 1)):
            parts[s - 1] = parts[s - 1] + chip_shift(parts[s].astype(BF), -1).astype(F32)
        return parts

    def give_back(parts):
        total = parts[0] + chip_shift(parts[1].astype(BF), -1).astype(F32)
        if chips > 2:
            total = total + chip_shift(parts[chips - 1].astype(BF), 1).astype(F32)
        return total

    h = {0: hidden, 1: chip_shift(hidden, 1)}
    if chips > 2:
        h[chips - 1] = chip_shift(hidden, -1)
    for s in range(2, chips - 1):
        h[s] = chip_shift(h[s - 1], 1)
    h[0], h[chips - 1] = after((h[0], h[chips - 1]), h[chips - 1], gate_w, up_w)
    h[1] = after(h[1], h[chips - 1])
    first, second = (list(range(chips - 2, 0, -1)), [chips - 1, 0]) if chips > 2 else ([1, 0], [])
    hs, ts, fed, partials = [], [], [], {}
    for part in (first, second):
        if not part:
            continue
        h_pair, t_pair = both([h[s] for s in part]), both([t[s] for s in part])
        if partials:
            h_pair = after(h_pair, mine)
        *kept, mine, other = feed(h_pair, t_pair, gate_w, up_w, down)
        mine = mine + core_swap(other).astype(F32)
        partials.update({s: mine[i] for i, s in enumerate(part)})
        flat = lambda arrays: [one.reshape(len(part) * rows, -1) for one in arrays]
        hs, ts = hs + flat(h_pair), ts + flat(t_pair)
        fed.append(flat(kept))
    acts, dgates, dups = ([one for kept in fed for one in kept[i::3]] for i in range(3))
    partials = pass_back(partials)
    hs = after(hs, partials)
    grad_hidden = give_back(partials)

    grad_gu = gate_up_grads(blocks, packs, depth, ff, hs, dgates, dups)
    out_parts, outs = [matmul(act, down) for act in after(acts, grad_gu)], {}
    for i, part in enumerate((first, second)):
        if part:
            other = core_swap(out_parts[2 * i + 1].astype(BF))
            mine = (out_parts[2 * i] + other.astype(F32)).reshape(len(part), rows, width)
            outs.update({s: mine[n] for n, s in enumerate(part)})
    grad_hidden = after(grad_hidden, grad_gu)

    grad_gu = after(grad_gu, normed_all, att_all).reshape(packs * blocks * 2 * depth, ff)
    grad_gu = lax.psum_scatter(grad_gu, "pack", scatter_dimension=0, tiled=True)

    _, second_pull = jax.vjp(rms_norm, middle, mlp_gain)
    grad_mid, grad_mlp_gain = second_pull(grad_hidden)
    grad_middle = grad_top.astype(F32) + grad_mid

    middle_low = grad_middle.astype(BF)

    dout = matmul_nt(middle_low, out_full).astype(BF).reshape(rows, q_cols)
    dout, outs = after((dout, outs), dout, outs)
    outs = pass_back(outs)
    if chips > 2:
        outs[chips - 1] = chip_shift(outs[chips - 1].astype(BF), 1)
    dq, dk0, dv0, dk1, dv1 = attention_backward(
        meta, qkv, dout, att, lse, starts, kv_line, kv_other, cosine, sine
    )
    dk1, dv1, outs = after((dk1, dv1, outs), outs)
    result = middle + outs[0] + chip_shift(outs[1].astype(BF), -1).astype(F32)
    if chips > 2:
        result = result + outs[chips - 1].astype(F32)
    result = result.astype(BF)
    other = core_swap(jnp.concatenate([dk1, dv1], axis=2))
    mine = jnp.concatenate([dk0, dv0], axis=2).astype(F32) + other.astype(F32)
    acts, ts = after((acts, ts), mine)
    grad_down = down_grads(acts, ts)
    sent = [by_columns(middle_low, packs), by_columns(after(dq, grad_down), packs)]
    got = exchange_packs(place, jnp.concatenate(sent, axis=2))
    got = jnp.concatenate(in_pack_order(place, got))
    part = width // packs
    parts = [matmul_tn(att_all, got[:, :part]), matmul_tn(normed_all, got[:, part:])]
    parts = jnp.concatenate(parts, axis=1).astype(BF)
    pair = mine[0]
    for s in range(1, chips):
        pair = pair + chip_shift(mine[s].astype(BF), -s, cyclic=False).astype(F32)
    turned = []
    for j in range(KVH):
        one = pair[:, j * HD : (j + 1) * HD]
        swapped = jnp.concatenate([one[:, half:], one[:, :half]], axis=1)
        turned.append(one * cosine - swapped * sine)
    dkv = jnp.concatenate(turned + [pair[:, KVH * HD :]], axis=1).astype(BF)
    gu_here = exchange_chips(place, grad_gu.reshape(chips, 2, 2, depth, ff))
    parts = reduce_line(place, parts.reshape(chips, 2, packs * depth, -1), gu_here).astype(BF)
    gu_here = exchange_cores(place, gu_here)
    parts = after(parts, dkv, result)
    got = exchange_packs(place, parts.reshape(packs, depth, -1))
    got = in_pack_order(place, got)
    grad_out_w = jnp.concatenate([piece[:, :part] for piece in got], axis=1).astype(F32)
    grad_q = jnp.concatenate([piece[:, part:] for piece in got], axis=1).astype(F32)
    grad_down = lax.psum_scatter(grad_down, "pack", scatter_dimension=0, tiled=True).astype(F32)
    grad_gu = gu_here.reshape(blocks, 2, depth, ff).transpose(1, 2, 0, 3).reshape(2, depth, -1)
    grad_gate_w, grad_up_w = grad_gu[0].astype(F32), grad_gu[1].astype(F32)
    dproj = jnp.concatenate([dq, dkv], axis=1)

    grad_normed = matmul_nt(dproj, qkv_full)
    _, first_pull = jax.vjp(rms_norm, stream, attn_gain)
    grad_input, grad_attn_gain = first_pull(grad_normed)
    input_grad = (grad_middle + grad_input).astype(BF)
    grad_bias = jnp.sum(dproj.astype(F32), axis=0)
    vector_grads = jnp.concatenate(
        [
            grad_bias.reshape(-1, bias_n),
            grad_attn_gain.reshape(-1, gain_n),
            grad_mlp_gain.reshape(-1, gain_n),
        ],
        axis=1,
    ).astype(BF)
    part = (qkv_cols - q_cols) // packs
    lines = -(-vector_grads.shape[1] // part)
    lines += -(blocks * lines) % 16 // blocks
    vector_grads = jnp.pad(vector_grads, ((0, 0), (0, lines * part - vector_grads.shape[1])))
    vector_grads = vector_grads.reshape(blocks, packs, lines, part).transpose(1, 0, 2, 3)
    vector_grads = vector_grads.reshape(packs, blocks * lines, part)
    got = exchange_packs(place, jnp.concatenate([by_columns(dkv, packs), vector_grads], axis=1))
    kv_all = jnp.concatenate(in_pack_order(place, [piece[:rows] for piece in got]))
    grad_kv = matmul_tn(normed_all, kv_all).astype(BF)
    vector_sum = sum(piece[rows:].astype(F32) for piece in got).astype(BF)
    grad_kv = jnp.concatenate(
        [grad_kv.reshape(blocks, packs * depth, part), vector_sum.reshape(blocks, lines, part)],
        axis=1,
    )
    grad_kv = reduce_line(place, grad_kv.reshape(chips, 2, -1, part))
    tail = grad_kv[packs * depth :].reshape(-1)
    grad_kv = to_shard(place, grad_kv[: packs * depth].astype(BF), depth)
    return (
        result[None],
        input_grad[None],
        jnp.concatenate([grad_q, grad_kv], axis=1),
        tail[:bias_n],
        grad_out_w,
        tail[bias_n : bias_n + gain_n],
        grad_gate_w,
        grad_up_w,
        grad_down,
        tail[bias_n + gain_n : bias_n + 2 * gain_n],
    )


def solution(mesh):
    tokens, rows, vector = P("pack", "blk", None), P(BOTH, None), P(BOTH)
    in_specs = (
        tokens, P("pack", None), tokens, rows, vector, rows, vector, rows, rows, rows, vector
    )
    out_specs = (tokens, tokens, rows, vector, rows, vector, rows, rows, rows, vector)
    return jax.shard_map(
        on_device, mesh=mesh, in_specs=in_specs, out_specs=out_specs, check_vma=False
    )
```

```python
import functools

import jax
import jax.numpy as jnp
from jax import lax
from jax.experimental import pallas as pl
from jax.experimental.pallas import tpu as pltpu
from jax.sharding import PartitionSpec as P

H = 12
KVH = 2
HD = 128
G = H // KVH
NEG = -1e30
BF = jnp.bfloat16
F32 = jnp.float32
VMEM_LIMIT = 56 * 1024 * 1024
BOTH = ("blk", "pack")


def chip_shift(block, by, cyclic=True):
    n = lax.axis_size("blk")
    route = [(i, (i + 2 * by) % n) for i in range(n) if cyclic or 0 <= i + 2 * by < n]
    return lax.ppermute(block, "blk", route)


def core_swap(block):
    n = lax.axis_size("blk")
    return lax.ppermute(block, "blk", [(i, i ^ 1) for i in range(n)])


def pack_swap(block, k):
    n = lax.axis_size("pack")
    return lax.ppermute(block, "pack", [(i, i ^ k) for i in range(n)])


def put(buffer, piece, *index):
    piece = piece.reshape((1,) * len(index) + piece.shape)
    zeros = (0,) * (buffer.ndim - len(index))
    return lax.dynamic_update_slice(buffer, piece, tuple(index) + zeros)


def take(array, axis, index):
    return lax.dynamic_index_in_dim(array, index, axis, keepdims=False)


class Place:
    def __init__(self):
        self.blocks, self.packs = lax.axis_size("blk"), lax.axis_size("pack")
        self.chips = self.blocks // 2
        self.blk, self.pack = lax.axis_index("blk"), lax.axis_index("pack")
        self.chip, self.core = self.blk // 2, self.blk % 2

    def chip_at(self, by):
        return lax.rem(self.chip + by + self.chips, self.chips)


def in_core_order(place, mine, other):
    first = jnp.where(place.core == 0, mine, other)
    second = jnp.where(place.core == 0, other, mine)
    return jnp.stack([first, second], axis=1)


def after(value, *before):
    return lax.optimization_barrier((value, before))[0]


def gather_line(block):
    chips = lax.axis_size("blk") // 2
    return jnp.stack([block] + [chip_shift(block, s) for s in range(1, chips)])


def exchange_packs(place, parts):
    got = [take(parts, 0, place.pack)]
    for k in range(1, place.packs):
        got.append(pack_swap(take(parts, 0, place.pack ^ k), k))
    return got


def reduce_line(place, parts, before=()):
    other = core_swap(take(parts, 1, 1 - place.core))
    mine = after(take(parts, 1, place.core).astype(F32) + other.astype(F32), before)
    line = mine.astype(BF)
    total = take(mine, 0, place.chip)
    for s in range(1, place.chips):
        total = total + chip_shift(take(line, 0, place.chip_at(s)), s).astype(F32)
    return total


def by_columns(matrix, packs):
    return jnp.stack(jnp.split(matrix, packs, axis=1))


def in_pack_order(place, pieces):
    ordered = []
    for q in range(place.packs):
        chosen = pieces[q]
        for p in range(1, place.packs):
            chosen = jnp.where(place.pack == p, pieces[q ^ p], chosen)
        ordered.append(chosen)
    return ordered


def to_shard(place, grad, depth):
    pieces = exchange_packs(place, grad.reshape(place.packs, depth, -1))
    return jnp.concatenate(in_pack_order(place, pieces), axis=1).astype(F32)


def exchange_chips(place, parts):
    got = jnp.zeros(parts.shape, parts.dtype)
    got = put(got, take(parts, 0, place.chip), place.chip)
    for s in range(1, place.chips):
        got = put(got, chip_shift(take(parts, 0, place.chip_at(s)), s), place.chip_at(-s))
    return got


def exchange_cores(place, got):
    other = core_swap(take(got, 1, 1 - place.core))
    return in_core_order(place, take(got, 1, place.core), other)


def matmul(left, right):
    return jnp.dot(left, right, preferred_element_type=F32)


def matmul_tn(left, right):
    return lax.dot_general(left, right, (((0,), (0,)), ((), ())), preferred_element_type=F32)


def matmul_nt(left, right):
    return lax.dot_general(left, right, (((1,), (1,)), ((), ())), preferred_element_type=F32)


def rms_norm(values, gain):
    return values * lax.rsqrt(jnp.mean(values * values, axis=-1, keepdims=True) + 1e-06) * gain


def turn(x, cosine, sine):
    return x * cosine + pltpu.roll(x, HD // 2, 1) * sine


def qkv_kernel(xn_ref, w_ref, bias_ref, cos_ref, sin_ref, out_ref):
    step = pl.program_id(0)
    proj = matmul(xn_ref[...], w_ref[...]) + bias_ref[...]
    cosine, sine = cos_ref[...], sin_ref[...]

    @pl.when(step < H // 2)
    def _():
        for i in range(2):
            cut = slice(i * HD, (i + 1) * HD)
            out_ref[:, cut] = (turn(proj[:, cut], cosine, sine) * HD**-0.5).astype(BF)

    @pl.when((step >= H // 2) & (step < (H + KVH) // 2))
    def _():
        for i in range(2):
            cut = slice(i * HD, (i + 1) * HD)
            out_ref[:, cut] = turn(proj[:, cut], cosine, sine).astype(BF)

    @pl.when(step >= (H + KVH) // 2)
    def _():
        out_ref[...] = proj.astype(BF)


def qkv_project(xn, w, bias, cosine, sine):
    rows, depth = xn.shape
    cols = w.shape[1]
    return pl.pallas_call(
        qkv_kernel,
        grid=(cols // 256,),
        in_specs=[
            pl.BlockSpec((rows, depth), lambda i: (0, 0)),
            pl.BlockSpec((depth, 256), lambda i: (0, i)),
            pl.BlockSpec((1, 256), lambda i: (0, i)),
            pl.BlockSpec((rows, HD), lambda i: (0, 0)),
            pl.BlockSpec((rows, HD), lambda i: (0, 0)),
        ],
        out_specs=pl.BlockSpec((rows, 256), lambda i: (0, i)),
        out_shape=jax.ShapeDtypeStruct((rows, cols), BF),
        compiler_params=pltpu.CompilerParams(vmem_limit_bytes=VMEM_LIMIT),
        cost_estimate=pl.CostEstimate(
            flops=2 * rows * depth * cols, bytes_accessed=2 * depth * cols, transcendentals=0
        ),
    )(xn, w, bias, cosine, sine)


def allowed_mask(meta_ref, starts_ref, slot, count):
    rows, lanes = starts_ref.shape[1], G * starts_ref.shape[1]
    starts = jnp.concatenate([starts_ref[...]] * G, axis=1)
    key_index = meta_ref[1 + count + slot] + lax.broadcasted_iota(jnp.int32, (rows, lanes), 0)
    query = lax.rem(lax.broadcasted_iota(jnp.int32, (1, lanes), 1), rows)
    return (key_index >= starts) & (key_index <= meta_ref[0] + query)


def stack_heads(target, source_ref):
    rows = source_ref.shape[0]
    for g in range(G):
        target[g * rows : (g + 1) * rows, :] = source_ref[:, g * HD : (g + 1) * HD]


def when_needed(meta_ref, count, work, pieces):
    slot = pl.program_id(1)
    state = meta_ref[1 + slot]
    for core, (k_ref, v_ref) in enumerate(pieces):
        here = slot < count // 2 if core == 0 else slot >= count // 2
        for masked in (True, False):

            @pl.when(here & (state == (1 if masked else 2)))
            def _(k_ref=k_ref, v_ref=v_ref, masked=masked):
                work(k_ref[0], v_ref[0], masked)


def forward_kernel(
    count, meta_ref, q_ref, starts_ref, k0_ref, v0_ref, k1_ref, v1_ref,
    att_ref, low_ref, lse_ref, q, m, total, acc,
):
    slot = pl.program_id(1)
    rows = q_ref.shape[0]

    @pl.when(slot == 0)
    def _():
        stack_heads(q, q_ref)
        m[...] = jnp.full(m.shape, NEG, F32)
        total[...] = jnp.zeros(total.shape, F32)
        acc[...] = jnp.zeros(acc.shape, F32)

    def work(keys, values, masked):
        scores = matmul_nt(keys, q[...])
        if masked:
            scores = jnp.where(allowed_mask(meta_ref, starts_ref, slot, count), scores, NEG)
        before = m[...]
        now = jnp.maximum(before, jnp.max(scores, axis=0, keepdims=True))
        weights = jnp.exp(scores - now)
        fade = jnp.exp(before - now)
        m[...] = now
        total[...] = total[...] * fade + jnp.sum(weights, axis=0, keepdims=True)
        acc[...] = acc[...] * fade + matmul_tn(values, weights.astype(BF))

    when_needed(meta_ref, count, work, ((k0_ref, v0_ref), (k1_ref, v1_ref)))

    @pl.when(slot == count - 1)
    def _():
        out = acc[...] / total[...]
        for g in range(G):
            head = out[:, g * rows : (g + 1) * rows].T
            att_ref[:, g * HD : (g + 1) * HD] = head
            low_ref[:, g * HD : (g + 1) * HD] = head.astype(BF)
        lse_ref[0] = m[...] + jnp.log(total[...])


def kv_specs(count, rows):
    half = count // 2
    specs = []
    for core in range(2):
        for first in (0, KVH):

            def where(h, j, meta_ref, core=core, first=first):
                here = (j < half) if core == 0 else (j >= half)
                index = jnp.where(here & (meta_ref[1 + j] > 0), j - core * half, 0)
                return (index, 0, first + h)

            specs.append(pl.BlockSpec((1, rows, HD), where))
    return specs


def attention_forward(meta, qkv, starts, line, other):
    count, rows = 2 * line.shape[0], line.shape[1]
    width = G * HD
    by_head = lambda h, j, meta_ref: (0, h)
    return pl.pallas_call(
        functools.partial(forward_kernel, count),
        grid_spec=pltpu.PrefetchScalarGridSpec(
            num_scalar_prefetch=1,
            grid=(KVH, count),
            in_specs=[
                pl.BlockSpec((rows, width), by_head),
                pl.BlockSpec((1, rows), lambda h, j, meta_ref: (0, 0)),
            ]
            + kv_specs(count, rows),
            out_specs=[
                pl.BlockSpec((rows, width), by_head),
                pl.BlockSpec((rows, width), by_head),
                pl.BlockSpec((1, 1, G * rows), lambda h, j, meta_ref: (h, 0, 0)),
            ],
            scratch_shapes=[
                pltpu.VMEM((G * rows, HD), BF),
                pltpu.VMEM((1, G * rows), F32),
                pltpu.VMEM((1, G * rows), F32),
                pltpu.VMEM((HD, G * rows), F32),
            ],
        ),
        out_shape=[
            jax.ShapeDtypeStruct((rows, H * HD), F32),
            jax.ShapeDtypeStruct((rows, H * HD), BF),
            jax.ShapeDtypeStruct((KVH, 1, G * rows), F32),
        ],
        compiler_params=pltpu.CompilerParams(vmem_limit_bytes=VMEM_LIMIT),
        cost_estimate=pl.CostEstimate(
            flops=16 * rows * rows * count * H * HD,
            bytes_accessed=count * rows * 1024,
            transcendentals=rows * rows * count * H,
        ),
    )(meta, qkv, starts, line, line, other, other)


def backward_kernel(
    count, meta_ref, q_ref, dout_ref, att_ref, lse_ref, starts_ref, k0_ref, v0_ref, k1_ref, v1_ref,
    cos_ref, sin_ref, dq_ref, dk0_ref, dv0_ref, dk1_ref, dv1_ref, q, dout, delta, dq_sum,
):
    slot = pl.program_id(1)
    rows = q_ref.shape[0]
    half = count // 2

    @pl.when(slot == 0)
    def _():
        stack_heads(q, q_ref)
        stack_heads(dout, dout_ref)
        dq_sum[...] = jnp.zeros(dq_sum.shape, F32)
        for g in range(G):
            cut = slice(g * HD, (g + 1) * HD)
            product = dout_ref[:, cut].astype(F32) * att_ref[:, cut]
            delta[:, g * rows : (g + 1) * rows] = jnp.sum(product.T, axis=0, keepdims=True)

    def work(keys, values, masked):
        weights = jnp.exp(matmul_nt(keys, q[...]) - lse_ref[0])
        if masked:
            weights = jnp.where(allowed_mask(meta_ref, starts_ref, slot, count), weights, 0.0)
        dv = matmul(weights.astype(BF), dout[...]).astype(BF)
        dscores = (weights * (matmul_nt(values, dout[...]) - delta[...])).astype(BF)
        dk = matmul(dscores, q[...]).astype(BF)
        dq_sum[...] = dq_sum[...] + matmul_tn(keys, dscores)

        @pl.when(slot < half)
        def _():
            dk0_ref[0], dv0_ref[0] = dk, dv

        @pl.when(slot >= half)
        def _():
            dk1_ref[0], dv1_ref[0] = dk, dv

    @pl.when((meta_ref[1 + slot] == 0) & (slot < half))
    def _():
        dk0_ref[...] = jnp.zeros(dk0_ref.shape, BF)
        dv0_ref[...] = jnp.zeros(dv0_ref.shape, BF)

    @pl.when((meta_ref[1 + slot] == 0) & (slot >= half))
    def _():
        dk1_ref[...] = jnp.zeros(dk1_ref.shape, BF)
        dv1_ref[...] = jnp.zeros(dv1_ref.shape, BF)

    when_needed(meta_ref, count, work, ((k0_ref, v0_ref), (k1_ref, v1_ref)))

    @pl.when(slot == count - 1)
    def _():
        for g in range(G):
            back = dq_sum[:, g * rows : (g + 1) * rows].T * HD**-0.5
            dq_ref[:, g * HD : (g + 1) * HD] = turn(back, cos_ref[...], -sin_ref[...]).astype(BF)


def attention_backward(meta, qkv, dout, att, lse, starts, line, other, cosine, sine):
    chips, rows = line.shape[:2]
    count = 2 * chips
    width = G * HD
    whole = lambda h, j, meta_ref: (0, 0)
    by_head = lambda h, j, meta_ref: (0, h)
    own = pl.BlockSpec((1, rows, HD), lambda h, j, meta_ref: (jnp.minimum(j, chips - 1), 0, h))
    far = pl.BlockSpec((1, rows, HD), lambda h, j, meta_ref: (jnp.maximum(j - chips, 0), 0, h))
    return pl.pallas_call(
        functools.partial(backward_kernel, count),
        grid_spec=pltpu.PrefetchScalarGridSpec(
            num_scalar_prefetch=1,
            grid=(KVH, count),
            in_specs=[
                pl.BlockSpec((rows, width), by_head),
                pl.BlockSpec((rows, width), by_head),
                pl.BlockSpec((rows, width), by_head),
                pl.BlockSpec((1, 1, G * rows), lambda h, j, meta_ref: (h, 0, 0)),
                pl.BlockSpec((1, rows), whole),
            ]
            + kv_specs(count, rows)
            + [pl.BlockSpec((rows, HD), whole)] * 2,
            out_specs=[pl.BlockSpec((rows, width), by_head), own, own, far, far],
            scratch_shapes=[
                pltpu.VMEM((G * rows, HD), BF),
                pltpu.VMEM((G * rows, HD), BF),
                pltpu.VMEM((1, G * rows), F32),
                pltpu.VMEM((HD, G * rows), F32),
            ],
        ),
        out_shape=[jax.ShapeDtypeStruct((rows, H * HD), BF)]
        + [jax.ShapeDtypeStruct((chips, rows, KVH * HD), BF)] * 4,
        compiler_params=pltpu.CompilerParams(vmem_limit_bytes=VMEM_LIMIT),
        cost_estimate=pl.CostEstimate(
            flops=400 * rows * rows * count * H * HD,
            bytes_accessed=count * rows * 1024,
            transcendentals=rows * rows * count * H,
        ),
    )(meta, qkv, dout, att, lse, starts, line, line, other, other, cosine, sine)


def assemble_kernel(packs, depth, at_ref, *refs):
    *sources, out_ref, sems = refs
    chips = sources[0].shape[0]
    chip, core, pack = at_ref[0], at_ref[1], at_ref[2]
    copies = []
    for n, source in enumerate(sources):
        k, other = n // 2, n % 2
        for s in range(chips):
            place = lax.rem(chip - s + chips, chips) * 2 + (core ^ other)
            start = pl.multiple_of((place * packs + (pack ^ k)) * depth, depth)
            copies.append(
                pltpu.make_async_copy(
                    source.at[s, pl.ds(0, depth)],
                    out_ref.at[pl.ds(start, depth)],
                    sems.at[len(copies)],
                )
            )
    for copy in copies:
        copy.start()
    for copy in copies:
        copy.wait()


def assemble(place, lines, depth):
    chips, _, cols = lines[0].shape
    count = len(lines) * chips
    if depth % 16:
        out = jnp.zeros((count, depth, cols), lines[0].dtype)
        for n, line in enumerate(lines):
            for s in range(chips):
                where = (place.chip_at(-s) * 2 + (place.core ^ (n % 2))) * place.packs
                out = put(out, line[s, :depth], where + (place.pack ^ (n // 2)))
        return out.reshape(count * depth, cols)
    at = jnp.stack([place.chip, place.core, place.pack]).astype(jnp.int32)
    return pl.pallas_call(
        functools.partial(assemble_kernel, place.packs, depth),
        grid_spec=pltpu.PrefetchScalarGridSpec(
            num_scalar_prefetch=1,
            grid=(1,),
            in_specs=[pl.BlockSpec(memory_space=pl.ANY)] * len(lines),
            out_specs=pl.BlockSpec((count * depth, cols), lambda i, at_ref: (0, 0)),
            scratch_shapes=[pltpu.SemaphoreType.DMA((count,))],
        ),
        out_shape=jax.ShapeDtypeStruct((count * depth, cols), lines[0].dtype),
        compiler_params=pltpu.CompilerParams(vmem_limit_bytes=VMEM_LIMIT),
        cost_estimate=pl.CostEstimate(
            flops=0, bytes_accessed=4 * count * depth * cols, transcendentals=0
        ),
    )(at, *lines)


def feed_kernel(
    h0_ref, h1_ref, t0_ref, t1_ref, gate_ref, up_ref, down_ref, *refs
):
    act0_ref, dgate0_ref, dup0_ref, act1_ref, dgate1_ref, dup1_ref, own_ref, other_ref, h, t = refs[-10:]
    rows = h0_ref.shape[1]
    h[:rows], h[rows:] = h0_ref[0], h1_ref[0]
    t[:rows], t[rows:] = t0_ref[0], t1_ref[0]
    gate = matmul(h[...], gate_ref[...])
    up = matmul(h[...], up_ref[...])
    dact = matmul_nt(t[...], down_ref[...])
    sig = 1.0 / (1.0 + jnp.exp(-gate))
    silu = gate * sig
    act = (silu * up).astype(BF)
    dgate = (dact * up * (sig * (1.0 + gate * (1.0 - sig)))).astype(BF)
    dup = (dact * silu).astype(BF)
    act0_ref[0], act1_ref[0] = act[:rows], act[rows:]
    dgate0_ref[0], dgate1_ref[0] = dgate[:rows], dgate[rows:]
    dup0_ref[0], dup1_ref[0] = dup[:rows], dup[rows:]
    part = matmul_nt(dgate, gate_ref[...]) + matmul_nt(dup, up_ref[...])
    own_ref[0] = part[:rows]
    other_ref[0] = part[rows:].astype(BF)


def feed(hs, ts, gate_w, up_w, down):
    count, rows, width = hs[0].shape
    ff = gate_w.shape[1]
    entry = lambda i: (i, 0, 0)
    whole = lambda i: (0, 0)
    once = pl.Buffered(1)
    tokens = pl.BlockSpec((1, rows, width), entry)
    column = pl.BlockSpec((1, rows, ff), entry)
    return pl.pallas_call(
        feed_kernel,
        grid=(count,),
        in_specs=[tokens] * 4
        + [
            pl.BlockSpec((width, ff), whole, pipeline_mode=once),
            pl.BlockSpec((width, ff), whole, pipeline_mode=once),
            pl.BlockSpec((ff, width), whole, pipeline_mode=once),
        ],
        out_specs=[column] * 6 + [tokens] * 2,
        out_shape=[jax.ShapeDtypeStruct((count, rows, ff), BF)] * 6
        + [
            jax.ShapeDtypeStruct((count, rows, width), F32),
            jax.ShapeDtypeStruct((count, rows, width), BF),
        ],
        scratch_shapes=[pltpu.VMEM((2 * rows, width), BF)] * 2,
        compiler_params=pltpu.CompilerParams(vmem_limit_bytes=VMEM_LIMIT),
        cost_estimate=pl.CostEstimate(
            flops=75 * count * rows * width * ff,
            bytes_accessed=6 * width * ff,
            transcendentals=2 * count * rows * ff,
        ),
    )(*hs, *ts, gate_w, up_w, down)


def grads_kernel(packs, n, *refs):
    *refs, out_ref = refs
    _, near, _, depth, ff = out_ref.shape
    for i in range(2):
        grad = sum(matmul_tn(refs[j][...], refs[n + i * n + j][...]) for j in range(n))
        grad = grad.astype(BF).reshape(near, packs, depth, ff)
        for p in range(packs):
            out_ref[p, :, i] = grad[:, p]


def gate_up_grads(blocks, packs, depth, ff, hs, dgates, dups):
    width = hs[0].shape[1]
    tile = width // 4
    if depth % 16 or tile % (packs * depth):
        grads = [sum(matmul_tn(h, d) for h, d in zip(hs, ds)).astype(BF) for ds in (dgates, dups)]
        return jnp.stack(grads).reshape(2, blocks, packs, depth, ff).transpose(2, 1, 0, 3, 4)
    near = tile // (packs * depth)
    columns = [pl.BlockSpec((h.shape[0], tile), lambda j: (0, j)) for h in hs]
    once = pl.Buffered(1)
    kept = [pl.BlockSpec(d.shape, lambda j: (0, 0), pipeline_mode=once) for d in dgates + dups]
    rows = sum(h.shape[0] for h in hs)
    return pl.pallas_call(
        functools.partial(grads_kernel, packs, len(hs)),
        grid=(4,),
        in_specs=columns + kept,
        out_specs=pl.BlockSpec((packs, near, 2, depth, ff), lambda j: (0, j, 0, 0, 0)),
        out_shape=jax.ShapeDtypeStruct((packs, blocks, 2, depth, ff), BF),
        compiler_params=pltpu.CompilerParams(vmem_limit_bytes=VMEM_LIMIT),
        cost_estimate=pl.CostEstimate(
            flops=7 * rows * width * ff, bytes_accessed=6 * rows * ff, transcendentals=0
        ),
    )(*hs, *dgates, *dups)


def down_grads_kernel(n, *refs):
    *refs, out_ref = refs
    out_ref[...] = sum(matmul_tn(refs[j][...], refs[n + j][...]) for j in range(n)).astype(BF)


def down_grads(acts, tops):
    ff, width = acts[0].shape[1], tops[0].shape[1]
    tile = width // 4
    rows = sum(act.shape[0] for act in acts)
    once = pl.Buffered(1)
    return pl.pallas_call(
        functools.partial(down_grads_kernel, len(acts)),
        grid=(4,),
        in_specs=[pl.BlockSpec(act.shape, lambda j: (0, 0), pipeline_mode=once) for act in acts]
        + [pl.BlockSpec((top.shape[0], tile), lambda j: (0, j)) for top in tops],
        out_specs=pl.BlockSpec((ff, tile), lambda j: (0, j)),
        out_shape=jax.ShapeDtypeStruct((ff, width), BF),
        compiler_params=pltpu.CompilerParams(vmem_limit_bytes=VMEM_LIMIT),
        cost_estimate=pl.CostEstimate(
            flops=2 * rows * width * ff, bytes_accessed=4 * rows * width, transcendentals=0
        ),
    )(*acts, *tops)


def on_device(
    tokens, lengths, out_grad, w_qkv, b_qkv, w_out, gain_attn, w_gate, w_up, w_down, gain_mlp
):
    rows, width = tokens.shape[1:]
    place = Place()
    blocks, packs, chips = place.blocks, place.packs, place.chips
    blk, chip, core = place.blk, place.chip, place.core
    depth = w_qkv.shape[0]
    qkv_cols = w_qkv.shape[1]
    ff = w_gate.shape[1] // blocks
    q_cols = H * HD

    token_index = blk * rows + jnp.arange(rows, dtype=jnp.int32)
    ends = jnp.cumsum(lengths[0])
    doc_starts = ends - lengths[0]
    inside = (token_index[:, None] >= doc_starts[None, :]) & (token_index[:, None] < ends[None, :])
    begin = jnp.sum(jnp.where(inside, doc_starts[None, :], 0), axis=1)
    half = HD // 2
    freq = 10000.0 ** (-2.0 * jnp.arange(half, dtype=F32) / HD)
    angle = (token_index - begin).astype(F32)[:, None] * freq[None, :]
    cosine, sine = jnp.cos(angle), jnp.sin(angle)
    cosine = jnp.concatenate([cosine, cosine], axis=1)
    sine = jnp.concatenate([-sine, sine], axis=1)
    starts = begin[None, :].astype(jnp.int32)

    bias_n, gain_n = b_qkv.shape[0], gain_attn.shape[0]
    shard = blk * packs + place.pack

    def placed(vector):
        row = jnp.zeros((qkv_cols,), BF)
        return lax.dynamic_update_slice(row, vector.astype(BF), (shard * vector.shape[0],))

    spare = jnp.stack([placed(b_qkv), placed(gain_attn), placed(gain_mlp)])
    spare = jnp.pad(spare, ((0, 5), (0, 0)))
    line = gather_line(jnp.concatenate([w_qkv.astype(BF), spare]))
    grad_top = out_grad[0]
    gate_up = jnp.stack([w_gate, w_up]).astype(BF).reshape(2, depth, chips, 2, ff)
    gate_up = after(gate_up.transpose(2, 3, 0, 1, 4), line)
    lines = [line] + [pack_swap(line, k) for k in range(1, packs)]
    lines = [piece for line in lines for piece in (line, core_swap(after(line, lines[1])))]
    gate_up = exchange_cores(place, after(exchange_chips(place, gate_up), lines))
    gate_up = gate_up.reshape(blocks, 2, depth, ff)
    vectors = jnp.sum(sum(piece[:, depth:].astype(F32) for piece in lines), axis=0)
    bias = vectors[:1]
    attn_gain, mlp_gain = vectors[1, :width], vectors[2, :width]
    out_line = gather_line(after(w_out.astype(BF), gate_up))
    qkv_full = assemble(place, lines, depth)

    down = lax.all_gather(after(w_down, lines[2]).astype(BF), "pack", axis=0, tiled=True)
    out_lines = [out_line] + [pack_swap(out_line, k) for k in range(1, packs)]

    def whole(part):
        part = lax.all_gather(part.reshape(blocks * depth, ff), "pack", axis=0, tiled=True)
        part = part.reshape(packs, blocks, depth, ff).transpose(1, 0, 2, 3)
        return part.reshape(width, ff)

    gate_w, up_w = whole(gate_up[:, 0]), whole(gate_up[:, 1])

    stream = tokens[0].astype(F32)
    normed = rms_norm(stream, attn_gain).astype(BF)
    top = after(out_grad[0], gate_up)
    t = {0: grad_top, 1: chip_shift(top, 1)}
    if chips > 2:
        t[chips - 1] = chip_shift(top, -1)
    qkv = qkv_project(after(normed, t), qkv_full, bias, cosine, sine)
    own = qkv[:, q_cols:]
    kv_line = jnp.stack([own] + [chip_shift(own, s, cyclic=False) for s in range(1, chips)])
    kv_other = core_swap(after(kv_line, out_lines))
    back = jnp.arange(chips, dtype=jnp.int32)
    source = jnp.concatenate([(chip - back) * 2 + core, (chip - back) * 2 + 1 - core])
    valid = ((source >= 0) & (source <= blk)).astype(jnp.int32)
    clear = ((source < blk) & (source * rows >= jnp.max(begin))).astype(jnp.int32)
    meta = jnp.concatenate([(blk * rows)[None], valid * (1 + clear), source * rows])
    meta = meta.astype(jnp.int32)
    att, att_low, lse = attention_forward(meta, qkv, starts, kv_line, kv_other)
    out_lines = after(out_lines, att_low)
    out_lines = [piece for line in out_lines for piece in (line, core_swap(line))]
    out_full = assemble(place, out_lines, depth)
    for s in range(2, chips - 1):
        t[s] = chip_shift(t[s - 1], 1)
    att_low = after(att_low, t)
    middle = stream + matmul(att_low, out_full)

    hidden = rms_norm(middle, mlp_gain).astype(BF)

    normed_all = lax.all_gather(after(normed, up_w, down), "pack", axis=0, tiled=True)
    att_all = lax.all_gather(after(att_low, up_w, down), "pack", axis=0, tiled=True)

    def both(blocks):
        line = jnp.stack(blocks)
        return line, core_swap(line)

    def pass_back(parts):
        parts = dict(parts)
        for s in reversed(range(2, chips - 1)):
            parts[s - 1] = parts[s - 1] + chip_shift(parts[s].astype(BF), -1).astype(F32)
        return parts

    def give_back(parts):
        total = parts[0] + chip_shift(parts[1].astype(BF), -1).astype(F32)
        if chips > 2:
            total = total + chip_shift(parts[chips - 1].astype(BF), 1).astype(F32)
        return total

    h = {0: hidden, 1: chip_shift(hidden, 1)}
    if chips > 2:
        h[chips - 1] = chip_shift(hidden, -1)
    for s in range(2, chips - 1):
        h[s] = chip_shift(h[s - 1], 1)
    h[0], h[chips - 1] = after((h[0], h[chips - 1]), h[chips - 1], gate_w, up_w)
    h[1] = after(h[1], h[chips - 1])
    first, second = (list(range(chips - 2, 0, -1)), [chips - 1, 0]) if chips > 2 else ([1, 0], [])
    hs, ts, fed, partials = [], [], [], {}
    for part in (first, second):
        if not part:
            continue
        h_pair, t_pair = both([h[s] for s in part]), both([t[s] for s in part])
        if partials:
            h_pair = after(h_pair, mine)
        *kept, mine, other = feed(h_pair, t_pair, gate_w, up_w, down)
        mine = mine + core_swap(other).astype(F32)
        partials.update({s: mine[i] for i, s in enumerate(part)})
        flat = lambda arrays: [one.reshape(len(part) * rows, -1) for one in arrays]
        hs, ts = hs + flat(h_pair), ts + flat(t_pair)
        fed.append(flat(kept))
    acts, dgates, dups = ([one for kept in fed for one in kept[i::3]] for i in range(3))
    partials = pass_back(partials)
    hs = after(hs, partials)
    grad_hidden = give_back(partials)

    grad_gu = gate_up_grads(blocks, packs, depth, ff, hs, dgates, dups)
    out_parts, outs = [matmul(act, down) for act in after(acts, grad_gu)], {}
    for i, part in enumerate((first, second)):
        if part:
            other = core_swap(out_parts[2 * i + 1].astype(BF))
            mine = (out_parts[2 * i] + other.astype(F32)).reshape(len(part), rows, width)
            outs.update({s: mine[n] for n, s in enumerate(part)})
    grad_hidden = after(grad_hidden, grad_gu)

    grad_gu = after(grad_gu, normed_all, att_all).reshape(packs * blocks * 2 * depth, ff)
    grad_gu = lax.psum_scatter(grad_gu, "pack", scatter_dimension=0, tiled=True)

    _, second_pull = jax.vjp(rms_norm, middle, mlp_gain)
    grad_mid, grad_mlp_gain = second_pull(grad_hidden)
    grad_middle = grad_top.astype(F32) + grad_mid

    middle_low = grad_middle.astype(BF)

    dout = matmul_nt(middle_low, out_full).astype(BF).reshape(rows, q_cols)
    dout, outs = after((dout, outs), dout, outs)
    outs = pass_back(outs)
    if chips > 2:
        outs[chips - 1] = chip_shift(outs[chips - 1].astype(BF), 1)
    dq, dk0, dv0, dk1, dv1 = attention_backward(
        meta, qkv, dout, att, lse, starts, kv_line, kv_other, cosine, sine
    )
    dk1, dv1, outs = after((dk1, dv1, outs), outs)
    result = middle + outs[0] + chip_shift(outs[1].astype(BF), -1).astype(F32)
    if chips > 2:
        result = result + outs[chips - 1].astype(F32)
    result = result.astype(BF)
    other = core_swap(jnp.concatenate([dk1, dv1], axis=2))
    mine = jnp.concatenate([dk0, dv0], axis=2).astype(F32) + other.astype(F32)
    acts, ts = after((acts, ts), mine)
    grad_down = down_grads(acts, ts)
    sent = [by_columns(middle_low, packs), by_columns(after(dq, grad_down), packs)]
    got = exchange_packs(place, jnp.concatenate(sent, axis=2))
    got = jnp.concatenate(in_pack_order(place, got))
    part = width // packs
    parts = [matmul_tn(att_all, got[:, :part]), matmul_tn(normed_all, got[:, part:])]
    parts = jnp.concatenate(parts, axis=1).astype(BF)
    pair = mine[0]
    for s in range(1, chips):
        pair = pair + chip_shift(mine[s].astype(BF), -s, cyclic=False).astype(F32)
    turned = []
    for j in range(KVH):
        one = pair[:, j * HD : (j + 1) * HD]
        swapped = jnp.concatenate([one[:, half:], one[:, :half]], axis=1)
        turned.append(one * cosine - swapped * sine)
    dkv = jnp.concatenate(turned + [pair[:, KVH * HD :]], axis=1).astype(BF)
    gu_here = exchange_chips(place, grad_gu.reshape(chips, 2, 2, depth, ff))
    parts = reduce_line(place, parts.reshape(chips, 2, packs * depth, -1), gu_here).astype(BF)
    gu_here = exchange_cores(place, gu_here)
    parts = after(parts, dkv, result)
    got = exchange_packs(place, parts.reshape(packs, depth, -1))
    got = in_pack_order(place, got)
    grad_out_w = jnp.concatenate([piece[:, :part] for piece in got], axis=1).astype(F32)
    grad_q = jnp.concatenate([piece[:, part:] for piece in got], axis=1).astype(F32)
    grad_down = lax.psum_scatter(grad_down, "pack", scatter_dimension=0, tiled=True).astype(F32)
    grad_gu = gu_here.reshape(blocks, 2, depth, ff).transpose(1, 2, 0, 3).reshape(2, depth, -1)
    grad_gate_w, grad_up_w = grad_gu[0].astype(F32), grad_gu[1].astype(F32)
    dproj = jnp.concatenate([dq, dkv], axis=1)

    grad_normed = matmul_nt(dproj, qkv_full)
    _, first_pull = jax.vjp(rms_norm, stream, attn_gain)
    grad_input, grad_attn_gain = first_pull(grad_normed)
    input_grad = (grad_middle + grad_input).astype(BF)
    grad_bias = jnp.sum(dproj.astype(F32), axis=0)
    vector_grads = jnp.concatenate(
        [
            grad_bias.reshape(-1, bias_n),
            grad_attn_gain.reshape(-1, gain_n),
            grad_mlp_gain.reshape(-1, gain_n),
        ],
        axis=1,
    ).astype(BF)
    part = (qkv_cols - q_cols) // packs
    lines = -(-vector_grads.shape[1] // part)
    lines += -(blocks * lines) % 16 // blocks
    vector_grads = jnp.pad(vector_grads, ((0, 0), (0, lines * part - vector_grads.shape[1])))
    vector_grads = vector_grads.reshape(blocks, packs, lines, part).transpose(1, 0, 2, 3)
    vector_grads = vector_grads.reshape(packs, blocks * lines, part)
    got = exchange_packs(place, jnp.concatenate([by_columns(dkv, packs), vector_grads], axis=1))
    kv_all = jnp.concatenate(in_pack_order(place, [piece[:rows] for piece in got]))
    grad_kv = matmul_tn(normed_all, kv_all).astype(BF)
    vector_sum = sum(piece[rows:].astype(F32) for piece in got).astype(BF)
    grad_kv = jnp.concatenate(
        [grad_kv.reshape(blocks, packs * depth, part), vector_sum.reshape(blocks, lines, part)],
        axis=1,
    )
    grad_kv = reduce_line(place, grad_kv.reshape(chips, 2, -1, part))
    tail = grad_kv[packs * depth :].reshape(-1)
    grad_kv = to_shard(place, grad_kv[: packs * depth].astype(BF), depth)
    return (
        result[None],
        input_grad[None],
        jnp.concatenate([grad_q, grad_kv], axis=1),
        tail[:bias_n],
        grad_out_w,
        tail[bias_n : bias_n + gain_n],
        grad_gate_w,
        grad_up_w,
        grad_down,
        tail[bias_n + gain_n : bias_n + 2 * gain_n],
    )


def solution(mesh):
    tokens, rows, vector = P("pack", "blk", None), P(BOTH, None), P(BOTH)
    in_specs = (
        tokens, P("pack", None), tokens, rows, vector, rows, vector, rows, rows, rows, vector
    )
    out_specs = (tokens, tokens, rows, vector, rows, vector, rows, rows, rows, vector)
    return jax.shard_map(
        on_device, mesh=mesh, in_specs=in_specs, out_specs=out_specs, check_vma=False
    )
```
